32 devices in a mesh: cell: 2 (over x), ap: 8 (over z, y), sc: 2 (over core).
Axes of the slice: x: 2, y: 2, z: 4, core: 2. Of those that a mesh axis runs over, the one named last changes fastest.
Arguments:
- unsmoothed_link_guesses: bfloat16 [32, 4, 2, 128, 2048], P(('cell', 'ap'), None, None, None, 'sc'), parts along dimension 0, may hold values from -24 to 24
- received: bfloat16 [32, 4, 2, 4, 2048], P(('cell', 'ap'), None, None, None, 'sc'), parts along dimension 0, may hold values from -6 to 6
- user_power: float32 [256], P('cell'), parts along dimension 0, may hold values from 0.25 to 4
- noise_power: float32 [32], P(('cell', 'ap')), parts along dimension 0, may hold values from 0.1 to 1
- ap_gain: float32 [32, 128], P(('cell', 'ap')), parts along dimension 0, may hold values from 0.5 to 4
- user_cluster: int32 [256], P('cell'), parts along dimension 0, may hold values from 0 to 15, as said below
- serving: int32 [32, 16], P('cell'), parts along dimension 0, may hold values from 0 to 1, as said below
- cluster_owner: int32 [32, 1], P('cell'), parts along dimension 0, may hold values from 0 to 7, as said below
Outputs:
- estimates: float32 [64, 8, 4, 2, 2048], P(('cell', 'ap'), None, None, None, 'sc'), parts along dimension 0
The draws below stay inside these ranges and needn't reach their ends.
There are 2 independent parts, one for each index of `cell`. The reference program is written for one: setup_inputs(seed, part) draws one part's arguments, and reference() takes and returns one part's arrays. A program takes and returns all parts, laid end to end along the dimension named above; each array names one. Nothing has to cross between parts.
Inputs may be any that keep to these rules, and one draw needn't show every extreme that they name: `user_cluster`: each of the 16 clusters holds exactly 8 users. `serving`: column a belongs to index a // 2 of ap. Where a cluster is served by an index of ap, at least one of its access points serves it. Of the clusters that one index of ap serves, at most 2 have the same owner; in every draw some owner has exactly 2 of its clusters served by every index of ap. `cluster_owner`: at most 4 clusters have the same owner, and some owner has exactly 4.
All inputs are finite; a program needn't handle non-finite values.
Results may differ from the reference program's by a relative error of at most 0.017.
Values may be sent and summed in bfloat16 or wider, within the bound.
No kernel may reach another device: no remote copies, remote signals or barrier semaphores. Data moves between devices by JAX's collectives and lax.ppermute only.
A program may use at most 128 MiB of HBM per device.

```python
import math
import jax
import jax.numpy as jnp
from jax import lax

AP_DEV = 2
ANTENNA_COUNT = 4
TONE_NUMBER = 2048
TAPS = 64
DATA_SYMBOLS = 4
CU = 8
OWN_MAX = 4
PEER_MAX = 2
ACCESS_POINTS = 16
CLUSTERS = 16
USER_TOTAL = 128
SLOTS = 32
N_AP = 8


def owner_and_serving(key):
    base_key = jax.random.fold_in(key, 11)
    subkeys = jax.random.split(base_key, 6)
    devices = ACCESS_POINTS // AP_DEV
    slot_count = devices * OWN_MAX
    heavy_owner = jax.random.randint(subkeys[0], (), 0, devices)
    slot_ids = jnp.arange(slot_count, dtype=jnp.int32)
    scores = jax.random.randint(subkeys[1], (slot_count,), 0, 1 << 16) * slot_count + slot_ids
    scores = jnp.where(slot_ids // OWN_MAX == heavy_owner, slot_ids - slot_count, scores)
    slot_order = jnp.argsort(scores)
    chosen = (slot_order[:CLUSTERS] // OWN_MAX).astype(jnp.int32)
    shuffled = jax.random.permutation(subkeys[2], CLUSTERS)
    owner_map = jnp.zeros((CLUSTERS,), jnp.int32).at[shuffled].set(chosen)
    cluster_ids = jnp.arange(CLUSTERS, dtype=jnp.int32)
    same_owner = owner_map[:, None] == owner_map[None, :]
    earlier = cluster_ids[None, :] < cluster_ids[:, None]
    cluster_rank = jnp.sum(same_owner & earlier, axis=1).astype(jnp.int32)
    coins = jax.random.randint(subkeys[3], (devices, CLUSTERS), 0, 2)
    before = jnp.sum(coins[:, None, :] * (same_owner & earlier).astype(jnp.int32)[None], axis=2)
    served = (coins == 1) & (before < PEER_MAX)
    device_ids = jnp.arange(devices, dtype=jnp.int32)
    turn_index = (cluster_rank[None, :] - device_ids[:, None]) % OWN_MAX
    forced = turn_index < PEER_MAX
    served = jnp.where((owner_map == heavy_owner)[None, :], forced, served)
    first_ap = jax.random.randint(subkeys[4], (devices, CLUSTERS), 0, AP_DEV)
    extra_bits = jax.random.randint(subkeys[5], (devices, CLUSTERS, AP_DEV), 0, 2)
    members = (extra_bits == 1) | (jnp.arange(AP_DEV, dtype=jnp.int32)[None, None, :] == first_ap[:, :, None])
    serving = (served[:, :, None] & members).astype(jnp.int32)
    serving = jnp.transpose(serving, (1, 0, 2)).reshape(CLUSTERS, ACCESS_POINTS)
    return (owner_map, serving)


def draw_cluster_owner(key, part):
    owner_map, serving = owner_and_serving(key)
    return owner_map[:, None].astype(jnp.int32)


def draw_serving(key, part):
    owner_map, serving = owner_and_serving(key)
    return serving.astype(jnp.int32)


def draw_user_cluster(key, part):
    shuffled = jax.random.permutation(jax.random.fold_in(key, 3), USER_TOTAL)
    return (shuffled // CU).astype(jnp.int32)


def level_of(stream_key, extent, cuts, smallest, top_value):
    gain, own = 1.0, jax.random.fold_in(stream_key, 6)
    for dim, shards_of in cuts:
        steps = jnp.exp(jax.random.uniform(jax.random.fold_in(own, dim), (shards_of,), jnp.float32, smallest / len(cuts), top_value / len(cuts)))
        gain = gain * jnp.repeat(steps, extent[dim] // shards_of).reshape([-1 if axis == dim else 1 for axis in range(len(extent))])
    return gain


def gaussian(stream_key, dims, deviation, most, shards=(), held_as=jnp.bfloat16):
    values = deviation * jax.random.normal(stream_key, dims, jnp.float32)
    if shards:
        values = values * level_of(stream_key, dims, shards, -0.22, 0.18)
    return jnp.clip(values, -most, most).astype(held_as)


def setup_inputs(seed: int = 0, part: int = 0) -> dict:
    seeds = jax.random.split(jax.random.key(seed), 9)
    part_keys = jax.random.split(jax.random.fold_in(seeds[8], part), 9)
    return {
        "unsmoothed_link_guesses": gaussian(part_keys[0], (ACCESS_POINTS, ANTENNA_COUNT, 2, USER_TOTAL, TONE_NUMBER), 4.0, 24.0, ((0, 8), (4, 2))),
        "received": gaussian(part_keys[1], (ACCESS_POINTS, ANTENNA_COUNT, 2, DATA_SYMBOLS, TONE_NUMBER), 1.0, 6.0, ((0, 8), (4, 2))),
        "user_power": jnp.clip(jnp.exp(jax.random.uniform(part_keys[2], (USER_TOTAL,), jnp.float32, math.log(0.25), math.log(4.0))), 0.25, 4.0),
        "noise_power": jnp.clip(jnp.exp(math.log(1.0) - 2.3025851 * jax.random.uniform(part_keys[3], (ACCESS_POINTS,), jnp.float32) ** level_of(part_keys[3], (ACCESS_POINTS,), ((0, 8),), -0.2, 0.2)), 0.1, 1.0),
        "ap_gain": jnp.clip(jnp.exp(math.log(4.0) - 2.0794415 * jax.random.uniform(part_keys[4], (ACCESS_POINTS, USER_TOTAL), jnp.float32) ** level_of(part_keys[4], (ACCESS_POINTS, USER_TOTAL), ((0, 8),), -0.2, 0.2)), 0.5, 4.0),
        "user_cluster": draw_user_cluster(jax.random.fold_in(jax.random.fold_in(seeds[8], part), 71), part),
        "serving": draw_serving(jax.random.fold_in(jax.random.fold_in(seeds[8], part), 71), part),
        "cluster_owner": draw_cluster_owner(jax.random.fold_in(jax.random.fold_in(seeds[8], part), 71), part),
    }


def complex_times(left_factor, right_factor):
    return (left_factor[0] * right_factor[0] - left_factor[1] * right_factor[1], left_factor[0] * right_factor[1] + left_factor[1] * right_factor[0])

def times_conj(left_factor, right_factor):
    return (left_factor[0] * right_factor[0] + left_factor[1] * right_factor[1], left_factor[1] * right_factor[0] - left_factor[0] * right_factor[1])

def hermitian_solve(cov_re, cov_im, right_re, right_im):
    dimension = cov_re.shape[0]
    factor = {}
    pivots = []
    for j in range(dimension):
        pivot_root = cov_re[j, j]
        for k in range(j):
            element = factor[j, k]
            pivot_root = pivot_root - (element[0] * element[0] + element[1] * element[1])
        pivot_root = jnp.sqrt(pivot_root)
        pivots.append(pivot_root)
        for i in range(j + 1, dimension):
            running = (cov_re[i, j], cov_im[i, j])
            for k in range(j):
                product = times_conj(factor[i, k], factor[j, k])
                running = (running[0] - product[0], running[1] - product[1])
            factor[i, j] = (running[0] / pivot_root, running[1] / pivot_root)
    forward = []
    for i in range(dimension):
        running = (right_re[i], right_im[i])
        for k in range(i):
            product = complex_times(factor[i, k], forward[k])
            running = (running[0] - product[0], running[1] - product[1])
        forward.append((running[0] / pivots[i], running[1] / pivots[i]))
    result = [None] * dimension
    for i in range(dimension - 1, -1, -1):
        running = forward[i]
        for k in range(i + 1, dimension):
            product = times_conj(result[k], factor[k, i])
            running = (running[0] - product[0], running[1] - product[1])
        result[i] = (running[0] / pivots[i], running[1] / pivots[i])
    return result

def lag_fourier_matrices(lowest_tone_hertz, tone_quantity):
    tone_hertz_values = lowest_tone_hertz + jnp.arange(tone_quantity, dtype=jnp.int32)
    lag_seconds = jnp.arange(TAPS, dtype=jnp.int32)
    rotation_angles = tone_hertz_values[:, None] * lag_seconds[None, :] % TONE_NUMBER
    angles = rotation_angles.astype(jnp.float32) * (2.0 * math.pi / TONE_NUMBER)
    return jnp.concatenate([jnp.cos(angles), jnp.sin(angles)], axis=1).astype(jnp.bfloat16)

def smoothing(h_group, lag_fourier_matrix):
    dims_shape = h_group.shape
    products = jnp.dot(h_group.reshape(-1, dims_shape[-1]), lag_fourier_matrix, preferred_element_type=jnp.float32)
    products = products.reshape(dims_shape[:-1] + (2 * TAPS,))
    coef_re = (products[:, :, 0, :, :TAPS] - products[:, :, 1, :, TAPS:]) / TONE_NUMBER
    coef_im = (products[:, :, 0, :, TAPS:] + products[:, :, 1, :, :TAPS]) / TONE_NUMBER
    return jnp.stack([coef_re, coef_im], axis=2)

def rebuild(coefficients, lag_fourier_matrix):
    coef_b = coefficients.astype(jnp.bfloat16)
    real_rows = jnp.concatenate([coef_b[:, :, 0], coef_b[:, :, 1]], axis=-1)
    imag_rows = jnp.concatenate([coef_b[:, :, 1], -coef_b[:, :, 0]], axis=-1)
    stacked = jnp.stack([real_rows, imag_rows], axis=2)
    dims_shape = stacked.shape
    smooth = jnp.dot(stacked.reshape(-1, 2 * TAPS), lag_fourier_matrix.T, preferred_element_type=jnp.float32)
    return smooth.reshape(dims_shape[:-1] + (lag_fourier_matrix.shape[0],))

def local_estimates(smooth, power_row, noise_level, right_side, weight_row):
    antennas = smooth.shape[0]
    scaled = smooth * (power_row / smooth.shape[2])[None, None, :, None]
    gram_sums = jnp.einsum('icuf,jduf->icjdf', scaled, smooth, precision=lax.Precision.HIGHEST)
    cov_re = gram_sums[:, 0, :, 0] + gram_sums[:, 1, :, 1] + noise_level * jnp.eye(antennas, dtype=smooth.dtype)[:, :, None]
    cov_im = gram_sums[:, 1, :, 0] - gram_sums[:, 0, :, 1]
    signal = right_side.astype(jnp.float32)
    solved = hermitian_solve(cov_re, cov_im, signal[:, 0], signal[:, 1])
    est_re = smooth[0, 0][:, None, :] * solved[0][0][None] + smooth[0, 1][:, None, :] * solved[0][1][None]
    est_im = smooth[0, 0][:, None, :] * solved[0][1][None] - smooth[0, 1][:, None, :] * solved[0][0][None]
    for i in range(1, antennas):
        est_re = est_re + smooth[i, 0][:, None, :] * solved[i][0][None] + smooth[i, 1][:, None, :] * solved[i][1][None]
        est_im = est_im + smooth[i, 0][:, None, :] * solved[i][1][None] - smooth[i, 1][:, None, :] * solved[i][0][None]
    return weight_row[:, None, None, None] * jnp.stack([est_re, est_im], axis=2)

def reference(unsmoothed_link_guesses, received, user_power, noise_power, ap_gain, user_cluster, serving, cluster_owner):
    lag_fourier_matrix = lag_fourier_matrices(0, TONE_NUMBER)
    cluster_ids = jnp.arange(CLUSTERS, dtype=jnp.int32)
    onehot = (user_cluster[:, None] == cluster_ids[None, :]).astype(jnp.float32)
    serve_user = jnp.dot(onehot, serving.astype(jnp.float32), precision=lax.Precision.HIGHEST)
    weights = serve_user.T * ap_gain
    totals = lax.optimization_barrier(jnp.sum(weights, axis=0))

    def group_step(carry, inputs):
        h_group, right_group, noise_group, weight_group = inputs
        smooth = rebuild(smoothing(h_group, lag_fourier_matrix), lag_fourier_matrix)
        partial_value = local_estimates(smooth[0], user_power, noise_group[0], right_group[0], weight_group[0])
        for station in range(1, AP_DEV):
            partial_value = partial_value + local_estimates(smooth[station], user_power, noise_group[station], right_group[station], weight_group[station])
        rounded = lax.optimization_barrier(partial_value.astype(jnp.bfloat16))
        return (carry + rounded.astype(jnp.float32), None)
    inputs = (unsmoothed_link_guesses.reshape((N_AP, AP_DEV) + unsmoothed_link_guesses.shape[1:]), received.reshape((N_AP, AP_DEV) + received.shape[1:]), noise_power.reshape(N_AP, AP_DEV), weights.reshape(N_AP, AP_DEV, USER_TOTAL))
    initial = jnp.zeros((USER_TOTAL, DATA_SYMBOLS, 2, TONE_NUMBER), jnp.float32)
    numerator, _ = lax.scan(group_step, initial, inputs)
    decoded = numerator / (1.0 + totals)[:, None, None, None]
    owner_map = cluster_owner[:, 0]
    cluster_rank = lax.optimization_barrier(jnp.sum((owner_map[:, None] == owner_map[None, :]) & (cluster_ids[None, :] < cluster_ids[:, None]), axis=1)).astype(jnp.int32)
    user_ids = jnp.arange(USER_TOTAL, dtype=jnp.int32)
    position = lax.optimization_barrier(jnp.sum((user_cluster[:, None] == user_cluster[None, :]) & (user_ids[None, :] < user_ids[:, None]), axis=1)).astype(jnp.int32)
    slot_index = (owner_map[user_cluster] * OWN_MAX + cluster_rank[user_cluster]).astype(jnp.int32)
    estimates = jnp.zeros((SLOTS, CU, DATA_SYMBOLS, 2, TONE_NUMBER), jnp.float32).at[slot_index, position].set(decoded)
    return estimates
```

```python
import functools
import math

import jax
import jax.numpy as jnp
import ml_dtypes
import numpy as np
from jax import lax
from jax.experimental import pallas as pl
from jax.experimental.pallas import tpu as pltpu
from jax.sharding import PartitionSpec as P

TONE_NUMBER = 2048
TAPS = 64
CU = 8
OWN_MAX = 4
PEER_MAX = 2
SAMPLES = 2 * TAPS
ROWS = PEER_MAX * CU
F32 = jnp.float32
BF16 = jnp.bfloat16


def np_parts(values, count):
    parts = []
    rest = values.astype(np.float64)
    for _ in range(count):
        part = rest.astype(np.float32).astype(ml_dtypes.bfloat16)
        parts.append(part)
        rest = rest - part.astype(np.float64)
    return parts


def np_angles(tones):
    turns = (tones[:, None] * np.arange(TAPS)[None, :]) % TONE_NUMBER
    return turns.astype(np.float64) * (2.0 * math.pi / TONE_NUMBER)


def forward_tables(shards, width):
    angles = np_angles(np.arange(shards * width))
    cosine = np.cos(angles).astype(np.float32).astype(ml_dtypes.bfloat16)
    sine = np.sin(angles).astype(np.float32).astype(ml_dtypes.bfloat16)
    real = np.concatenate([cosine, sine], axis=1).reshape(shards, width, 2 * TAPS)
    imag = np.concatenate([-sine, cosine], axis=1).reshape(shards, width, 2 * TAPS)
    return np.stack([real, imag], axis=1)


def rebuild_columns(tones):
    angles = np_angles(tones).T
    real = np.concatenate([np.cos(angles), np.sin(angles)], axis=0)
    imag = np.concatenate([-np.sin(angles), np.cos(angles)], axis=0)
    return (
        np.concatenate(np_parts(real, 2), axis=0),
        np.concatenate(np_parts(imag, 2), axis=0),
    )


def rebuild_tables(shards, width, chunk):
    real, imag = rebuild_columns(np.arange(shards * width))
    real = real.reshape(4 * TAPS, shards, width // chunk, 1, chunk)
    imag = imag.reshape(4 * TAPS, shards, width // chunk, 1, chunk)
    both = np.concatenate([real, imag], axis=3).reshape(4 * TAPS, shards, 2 * width)
    return np.ascontiguousarray(both.transpose(1, 0, 2))


def sample_table():
    real, imag = rebuild_columns(np.arange(SAMPLES) * (TONE_NUMBER // SAMPLES))
    return np.concatenate([real, imag], axis=1)


def dirichlet_tables(shards, width):
    step = TONE_NUMBER // SAMPLES
    wave = np.ones((TONE_NUMBER,), np.float64)
    tones = np.arange(TONE_NUMBER)
    for lag in range(1, TAPS):
        wave += 2.0 * np.cos(2.0 * math.pi * ((lag * tones) % TONE_NUMBER) / TONE_NUMBER)
    wave /= SAMPLES
    gap = (np.arange(shards * width)[None, :] - step * np.arange(SAMPLES)[:, None]) % TONE_NUMBER
    kernel = wave[gap]
    parts = np.concatenate(np_parts(kernel, 3), axis=0)
    parts = parts.reshape(3 * SAMPLES, shards, width)
    return np.ascontiguousarray(parts.transpose(1, 0, 2))


def coefficient_kernel(ids, table, guesses, out):
    antennas, _, users, tones = guesses.shape[1:]
    real = guesses[0, :, 0].reshape(antennas * users, tones)
    imag = guesses[0, :, 1].reshape(antennas * users, tones)
    total = jnp.dot(real, table[0, 0], preferred_element_type=F32)
    total = total + jnp.dot(imag, table[0, 1], preferred_element_type=F32)
    out[...] = (total * (1.0 / TONE_NUMBER)).astype(out.dtype)


def delay_coefficients(ids, guesses, shards):
    aps, antennas, _, users, tones = guesses.shape
    group = math.gcd(2, antennas)
    steps = antennas // group
    table = jnp.asarray(forward_tables(shards, tones))
    return pl.pallas_call(
        coefficient_kernel,
        grid_spec=pltpu.PrefetchScalarGridSpec(
            num_scalar_prefetch=1,
            grid=(aps, steps),
            in_specs=[
                pl.BlockSpec((1, 2, tones, 2 * TAPS), lambda a, i, ids: (ids[1], 0, 0, 0)),
                pl.BlockSpec((1, group, 2, users, tones), lambda a, i, ids: (a, i, 0, 0, 0)),
            ],
            out_specs=pl.BlockSpec(
                (group * users, 2 * TAPS), lambda a, i, ids: (a * steps + i, 0)
            ),
        ),
        out_shape=jax.ShapeDtypeStruct((aps * antennas * users, 2 * TAPS), BF16),
        compiler_params=pltpu.CompilerParams(vmem_limit_bytes=32 * 1024 * 1024),
        cost_estimate=pl.CostEstimate(
            flops=4 * guesses.size * 2 * TAPS // 2, bytes_accessed=2 * guesses.size, transcendentals=0
        ),
        name="delay_coefficients",
    )(ids, table, guesses)


def three_parts(values):
    high = values.astype(BF16)
    rest = values - high.astype(F32)
    middle = rest.astype(BF16)
    low = (rest - middle.astype(F32)).astype(BF16)
    return high, middle, low


def iota(shape, axis):
    return lax.broadcasted_iota(jnp.int32, shape, axis)


def column_of(row):
    n = row.shape[1]
    return jnp.sum(jnp.where(iota((n, n), 0) == iota((n, n), 1), row, 0.0), axis=1, keepdims=True)


def row_of(column):
    n = column.shape[0]
    return jnp.sum(
        jnp.where(iota((n, n), 0) == iota((n, n), 1), column, 0.0), axis=0, keepdims=True
    )


def payload_kernel(shape, ids, noise, *refs):
    aps, antennas, users, devices, shards = shape
    per = devices // shards
    parts = refs[:shards]
    power, gain, cluster_row, serving, owner, table = refs[shards : shards + 6]
    outs = refs[shards + 6 : shards + 6 + per]
    slots, coef, smooth, cov = refs[shards + 6 + per :]
    device, core = ids[0], ids[1]
    clusters = serving.shape[0]

    total = parts[0][...].astype(F32)
    for part in parts[1:]:
        total = total + part[...].astype(F32)
    coef_b = total.astype(BF16)
    coef[:, : 2 * TAPS] = coef_b
    coef[:, 2 * TAPS :] = coef_b

    smooth[...] = jnp.dot(coef[...], table[...], preferred_element_type=F32)
    scale = column_of(power[...]) * (1.0 / users)
    for a in range(aps):
        base = a * antennas * users
        sums = {}
        for start in range(0, users, 8):
            re, im = [], []
            for i in range(antennas):
                rows = smooth[pl.ds(base + i * users + start, 8), :]
                re.append(rows[:, :SAMPLES])
                im.append(rows[:, SAMPLES:])
            weight = jnp.broadcast_to(scale[start : start + 8], (8, SAMPLES))
            for i in range(antennas):
                sre, sim = re[i] * weight, im[i] * weight
                for j in range(i + 1):
                    value = sre * re[j] + sim * im[j]
                    sums[i, j, 0] = sums[i, j, 0] + value if start else value
                    if j < i:
                        value = sim * re[j] - sre * im[j]
                        sums[i, j, 1] = sums[i, j, 1] + value if start else value
        field = 0
        for i in range(antennas):
            for j in range(i + 1):
                for c in range(2 if j < i else 1):
                    row = jnp.sum(sums[i, j, c], axis=0, keepdims=True)
                    if i == j:
                        row = row + noise[a]
                    cov[pl.ds(a * antennas * antennas + field, 1), :] = row
                    field += 1

    serving_f = serving[...].astype(F32)
    columns = serving.shape[1]
    pairs = (iota((columns, devices), 0) // aps == iota((columns, devices), 1)).astype(F32)
    served = (jnp.dot(serving_f, pairs, preferred_element_type=F32) > 0.5).astype(F32)
    served_here = jnp.sum(
        jnp.where(iota((clusters, devices), 1) == device, served, 0.0), axis=1, keepdims=True
    )
    owner_col = owner[...]
    owner_f = owner_col.astype(F32)
    square = (clusters, clusters)
    before = iota(square, 1) < iota(square, 0)
    earlier = before & (owner_f == row_of(owner_f))
    turn = jnp.sum(jnp.where(earlier, row_of(served_here), 0.0), axis=1, keepdims=True)
    label = (owner_col ^ device) ^ (core * per)
    valid = (served_here > 0.5) & (label < per)
    base = jnp.where(valid, label.astype(F32) * ROWS + turn * CU, -4.0 * ROWS * devices)
    members = (iota((clusters, users), 0) == cluster_row[...]).astype(F32)
    prefix = (iota((users, users), 0) < iota((users, users), 1)).astype(F32)
    order = jnp.dot(members, prefix, preferred_element_type=F32)
    target = jnp.sum(members * (order + base), axis=0, keepdims=True).astype(jnp.int32)
    pick = (iota((per * ROWS, users), 0) == target).astype(F32).astype(BF16)

    weight_rows = []
    for a in range(aps):
        column = iota((clusters, columns), 1) == device * aps + a
        mine = jnp.sum(jnp.where(column, serving_f, 0.0), axis=1, keepdims=True)
        weight_rows.append(
            jnp.sum(members * mine, axis=0, keepdims=True) * gain[pl.ds(a, 1), :]
        )
    stacked = jnp.concatenate(
        weight_rows + [jnp.zeros((8 - aps, users), F32)], axis=0
    )
    weight_parts = jnp.concatenate(
        [part.astype(F32) for part in three_parts(stacked)]
        + [jnp.zeros((2 * TAPS - 24, users), F32)],
        axis=0,
    ).astype(BF16)
    picked_weights = lax.dot_general(
        pick, weight_parts, (((1,), (1,)), ((), ())), preferred_element_type=F32
    ).astype(BF16)

    cov_parts = three_parts(cov[...])
    cov_rows = cov.shape[0]
    first = aps * antennas * ROWS
    for ai in range(aps * antennas):
        chosen = jnp.dot(
            pick, coef[pl.ds(ai * users, users), : 2 * TAPS], preferred_element_type=F32
        ).astype(BF16)
        for j in range(per):
            outs[j][pl.ds(ai * ROWS, ROWS), :] = chosen[j * ROWS : (j + 1) * ROWS]
    for j in range(per):
        for k in range(3):
            outs[j][pl.ds(first + k * cov_rows, cov_rows), :] = cov_parts[k]
        outs[j][pl.ds(first + 3 * cov_rows, ROWS), :] = picked_weights[j * ROWS : (j + 1) * ROWS]

    mine = (owner_col == device).astype(F32)
    lower = before.astype(F32)
    rank = jnp.sum(jnp.where(before, row_of(mine), 0.0), axis=1, keepdims=True)
    here = mine * served
    turns = jnp.dot(lower, here, preferred_element_type=F32)
    for p in range(PEER_MAX):
        hit = jnp.where(turns == float(p), here, 0.0)
        slots[pl.ds(p, 1), :] = jnp.sum(hit * rank, axis=0, keepdims=True).astype(jnp.int32)


def payload_rows(aps, antennas):
    return aps * antennas * ROWS + 3 * aps * antennas * antennas + ROWS


def owner_payloads(ids, parts, power, noise, gain, cluster, serving, owner, shape):
    aps, antennas, users, devices, shards = shape
    per = devices // shards
    rows = payload_rows(aps, antennas)
    vmem = pl.BlockSpec(memory_space=pltpu.VMEM)
    smem = pl.BlockSpec(memory_space=pltpu.SMEM)
    return pl.pallas_call(
        functools.partial(payload_kernel, shape),
        in_specs=[smem, smem] + [vmem] * (shards + 6),
        out_specs=[vmem] * (per + 1),
        out_shape=[jax.ShapeDtypeStruct((rows, 2 * TAPS), BF16)] * per
        + [jax.ShapeDtypeStruct((PEER_MAX, devices), jnp.int32)],
        scratch_shapes=[
            pltpu.VMEM((aps * antennas * users, 4 * TAPS), BF16),
            pltpu.VMEM((aps * antennas * users, 2 * SAMPLES), F32),
            pltpu.VMEM((aps * antennas * antennas, SAMPLES), F32),
        ],
        compiler_params=pltpu.CompilerParams(vmem_limit_bytes=32 * 1024 * 1024),
        cost_estimate=pl.CostEstimate(
            flops=4 * aps * antennas * users * 4 * TAPS * SAMPLES,
            bytes_accessed=2 * 1024 * 1024,
            transcendentals=0,
        ),
        name="owner_payloads",
    )(
        ids,
        noise,
        *parts,
        power[None, :],
        gain,
        cluster[None, :],
        serving,
        owner,
        jnp.asarray(sample_table()),
    )


def complex_times(left, right):
    return (left[0] * right[0] - left[1] * right[1], left[0] * right[1] + left[1] * right[0])


def times_conj(left, right):
    return (left[0] * right[0] + left[1] * right[1], left[1] * right[0] - left[0] * right[1])


def minus(left, right):
    return (left[0] - right[0], left[1] - right[1])


def factorize(cov, antennas):
    factor, inverse = {}, []
    for j in range(antennas):
        pivot = cov[j, j][0]
        for k in range(j):
            pivot = pivot - (factor[j, k][0] * factor[j, k][0] + factor[j, k][1] * factor[j, k][1])
        root = lax.rsqrt(pivot)
        inverse.append(root)
        for i in range(j + 1, antennas):
            running = cov[i, j]
            for k in range(j):
                running = minus(running, times_conj(factor[i, k], factor[j, k]))
            factor[i, j] = (running[0] * root, running[1] * root)
    return factor, inverse


def substitute(factor, inverse, right):
    antennas = len(inverse)
    forward = []
    for i in range(antennas):
        running = right[i]
        for k in range(i):
            running = minus(running, complex_times(factor[i, k], forward[k]))
        forward.append((running[0] * inverse[i], running[1] * inverse[i]))
    result = [None] * antennas
    for i in range(antennas - 1, -1, -1):
        running = forward[i]
        for k in range(i + 1, antennas):
            running = minus(running, times_conj(result[k], factor[k, i]))
        result[i] = (running[0] * inverse[i], running[1] * inverse[i])
    return result


def estimate_kernel(shape, chunk, ids, slots, *refs):
    aps, antennas, symbols, tones, devices, shards = shape
    per = devices // shards
    pays, signals = refs[:devices], refs[devices : 2 * devices]
    kernel_table, rebuild_table, out = refs[2 * devices : 2 * devices + 3]
    (
        pay, sig, dirichlet, rebuild, left, cov_full, cov_tiles, sig_tiles, solved, smooth, weight,
        acc, denominator, turned, pay_sem, sig_sem, table_sem,
    ) = refs[2 * devices + 3 :]
    device, core = ids[0], ids[1]
    cov_rows = aps * antennas * antennas
    coef_rows = aps * antennas * ROWS
    blocks = tones // 128

    def copies():
        yield pltpu.make_async_copy(kernel_table.at[core], dirichlet, table_sem.at[0])
        for l in range(devices):
            yield pltpu.make_async_copy(pays[l], pay.at[l], pay_sem.at[l])
        yield pltpu.make_async_copy(rebuild_table.at[core], rebuild, table_sem.at[1])
        for v in range(devices):
            yield pltpu.make_async_copy(signals[v], sig.at[v], sig_sem.at[v])

    started = list(copies())
    for copy in started:
        copy.start()
    for copy in started:
        copy.wait()

    def cov_part(k):
        rows = pay[:, pl.ds(coef_rows + k * cov_rows, cov_rows), :]
        return rows.reshape(devices * cov_rows, SAMPLES)

    high, middle, low = cov_part(0), cov_part(1), cov_part(2)
    n = SAMPLES
    cov_full[...] = (
        jnp.dot(low, dirichlet[:n], preferred_element_type=F32)
        + jnp.dot(
            jnp.concatenate([middle, middle], axis=1), dirichlet[: 2 * n], preferred_element_type=F32
        )
        + jnp.dot(
            jnp.concatenate([high, high, high], axis=1), dirichlet[...], preferred_element_type=F32
        )
    )

    for l in range(devices):
        rows = pay[l, pl.ds(0, coef_rows), :]
        left[pl.ds(l * coef_rows, coef_rows), : 2 * TAPS] = rows
        left[pl.ds(l * coef_rows, coef_rows), 2 * TAPS :] = rows
        packed = pay[l, pl.ds(coef_rows + 3 * cov_rows, ROWS), :].astype(F32)
        for a in range(aps):
            value = packed[:, a : a + 1] + packed[:, 8 + a : 9 + a] + packed[:, 16 + a : 17 + a]
            weight[l, a] = jnp.broadcast_to(value, (ROWS, 128))

    acc[...] = jnp.zeros_like(acc)
    denominator[...] = jnp.ones_like(denominator)

    def label_of(l):
        return l ^ (core * per)

    def solve(l, carry):
        v = label_of(l)
        for r in range(0, cov_rows, 8):
            rows = cov_full[pl.ds(pl.multiple_of(l * cov_rows + r, 8), 8), :]
            for b in range(blocks):
                cov_tiles[pl.ds(r * blocks + b, 8, stride=blocks), :] = rows[:, b * 128 : (b + 1) * 128]
        for a in range(aps):
            for i in range(antennas):
                for c in range(2):
                    rows = sig[v, a, i, c].astype(F32)
                    first = ((a * antennas + i) * 2 + c) * symbols * blocks
                    for b in range(blocks):
                        sig_tiles[pl.ds(first + b, symbols, stride=blocks), :] = rows[
                            :, b * 128 : (b + 1) * 128
                        ]
        for a in range(aps):
            cov = {}
            field = a * antennas * antennas
            for i in range(antennas):
                for j in range(i + 1):
                    parts = []
                    for c in range(2 if j < i else 1):
                        parts.append(cov_tiles[pl.ds(field * blocks, blocks), :])
                        field += 1
                    cov[i, j] = parts
            factor, inverse = factorize(cov, antennas)
            for s in range(symbols):
                right = []
                for i in range(antennas):
                    tiles = [
                        (((a * antennas + i) * 2 + c) * symbols + s) * blocks for c in range(2)
                    ]
                    right.append([sig_tiles[pl.ds(t, blocks), :] for t in tiles])
                result = substitute(factor, inverse, right)
                for i in range(antennas):
                    for c in range(2):
                        at = ((a * antennas + i) * symbols + s) * 2 + c
                        solved[l, pl.ds(at * blocks, blocks), :] = result[i][c]
        for p in range(PEER_MAX):
            k = slots[p, v ^ device]
            for a in range(aps):
                denominator[k] = denominator[k] + weight[l, a, pl.ds(p * CU, CU), :]
        return carry

    lax.fori_loop(0, devices, solve, 0)

    def combine(l, q):
        v = label_of(l)
        for h in range(chunk // 128):
            b = q * (chunk // 128) + h
            lanes = pl.ds(pl.multiple_of(b * 128, 128), 128)
            totals = [[None] * (2 * symbols) for p in range(PEER_MAX)]
            for a in range(aps):
                for i in range(antennas):
                    base = pl.multiple_of(l * coef_rows + (a * antennas + i) * ROWS, 8)
                    link = []
                    for p in range(PEER_MAX):
                        scale = weight[l, a, pl.ds(p * CU, CU), :]
                        rows = pl.ds(base + p * CU, CU)
                        link.append(
                            (
                                smooth[rows, h * 128 : (h + 1) * 128] * scale,
                                smooth[rows, chunk + h * 128 : chunk + (h + 1) * 128] * scale,
                            )
                        )
                    for s in range(symbols):
                        at = ((a * antennas + i) * symbols + s) * 2
                        xr = solved[l, pl.ds(at * blocks + b, 1), :]
                        xi = solved[l, pl.ds((at + 1) * blocks + b, 1), :]
                        xr = jnp.broadcast_to(xr, (CU, 128))
                        xi = jnp.broadcast_to(xi, (CU, 128))
                        for p in range(PEER_MAX):
                            gr, gi = link[p]
                            er = gr * xr + gi * xi
                            ei = gr * xi - gi * xr
                            if totals[p][2 * s] is None:
                                totals[p][2 * s], totals[p][2 * s + 1] = er, ei
                            else:
                                totals[p][2 * s] += er
                                totals[p][2 * s + 1] += ei
            for p in range(PEER_MAX):
                k = slots[p, v ^ device]
                for e in range(2 * symbols):
                    acc[k, e, :, lanes] = acc[k, e, :, lanes] + totals[p][e]

    def one_chunk(q, carry):
        columns = pl.ds(pl.multiple_of(q * 2 * chunk, 128), 2 * chunk)
        smooth[...] = jnp.dot(left[...], rebuild[:, columns], preferred_element_type=F32)

        def step(l, inner):
            combine(l, q)
            return inner

        lax.fori_loop(0, devices, step, 0)
        return carry

    lax.fori_loop(0, tones // chunk, one_chunk, 0)

    def finish(k, carry):
        inverse = 1.0 / denominator[k]
        for b in range(blocks):
            for e in range(2 * symbols):
                value = acc[k, e, :, b * 128 : (b + 1) * 128] * inverse
                turned[pl.ds(b * CU * 2 * symbols + e, CU, stride=2 * symbols), :] = value
            for m in range(CU):
                for s in range(symbols):
                    at = ((b * CU + m) * symbols + s) * 2
                    out[k, m, s, :, b * 128 : (b + 1) * 128] = turned[pl.ds(at, 2), :]
        return carry

    lax.fori_loop(0, OWN_MAX, finish, 0)


def owner_estimates(ids, slots, pays, signals, shape):
    aps, antennas, symbols, tones, devices, shards = shape
    chunk = min(256, tones)
    rows = payload_rows(aps, antennas)
    cov_rows = aps * antennas * antennas
    coef_rows = aps * antennas * ROWS
    vmem = pl.BlockSpec(memory_space=pltpu.VMEM)
    smem = pl.BlockSpec(memory_space=pltpu.SMEM)
    anywhere = pl.BlockSpec(memory_space=pl.ANY)
    blocks = tones // 128
    return pl.pallas_call(
        functools.partial(estimate_kernel, shape, chunk),
        in_specs=[smem, smem] + [anywhere] * (2 * devices + 2),
        out_specs=vmem,
        out_shape=jax.ShapeDtypeStruct((OWN_MAX, CU, symbols, 2, tones), F32),
        scratch_shapes=[
            pltpu.VMEM((devices, rows, 2 * TAPS), BF16),
            pltpu.VMEM((devices,) + signals[0].shape, BF16),
            pltpu.VMEM((3 * SAMPLES, tones), BF16),
            pltpu.VMEM((4 * TAPS, 2 * tones), BF16),
            pltpu.VMEM((devices * coef_rows, 4 * TAPS), BF16),
            pltpu.VMEM((devices * cov_rows, tones), F32),
            pltpu.VMEM((cov_rows * blocks, 128), F32),
            pltpu.VMEM((aps * antennas * 2 * symbols * blocks, 128), F32),
            pltpu.VMEM((devices, aps * antennas * 2 * symbols * blocks, 128), F32),
            pltpu.VMEM((devices * coef_rows, 2 * chunk), F32),
            pltpu.VMEM((devices, aps, ROWS, 128), F32),
            pltpu.VMEM((OWN_MAX, 2 * symbols, CU, tones), F32),
            pltpu.VMEM((OWN_MAX, CU, 128), F32),
            pltpu.VMEM((CU * 2 * symbols * blocks, 128), F32),
            pltpu.SemaphoreType.DMA((devices,)),
            pltpu.SemaphoreType.DMA((devices,)),
            pltpu.SemaphoreType.DMA((2,)),
        ],
        compiler_params=pltpu.CompilerParams(vmem_limit_bytes=48 * 1024 * 1024),
        cost_estimate=pl.CostEstimate(
            flops=4 * devices * coef_rows * 4 * TAPS * tones,
            bytes_accessed=8 * 1024 * 1024,
            transcendentals=0,
        ),
        name="owner_estimates",
    )(
        ids,
        slots,
        *pays,
        *signals,
        jnp.asarray(dirichlet_tables(shards, tones)),
        jnp.asarray(rebuild_tables(shards, tones, chunk)),
    )


def local(
    unsmoothed_link_guesses,
    received,
    user_power,
    noise_power,
    ap_gain,
    user_cluster,
    serving,
    cluster_owner,
):
    aps, antennas, _, users, tones = unsmoothed_link_guesses.shape
    symbols = received.shape[3]
    devices, shards = lax.axis_size("ap"), lax.axis_size("sc")
    per = devices // shards
    ids = jnp.stack([lax.axis_index("ap"), lax.axis_index("sc")]).astype(jnp.int32)

    def swap_ap(value, v):
        return lax.ppermute(value, "ap", [(i, i ^ v) for i in range(devices)])

    def swap_sc(value, h):
        return lax.ppermute(value, "sc", [(c, c ^ h) for c in range(shards)])

    signals = [None] * devices
    for v in range(0, devices, 2):
        signals[v] = swap_ap(received, v) if v else received
        signals[v + 1] = swap_ap(signals[v], 1)

    combined = delay_coefficients(ids, unsmoothed_link_guesses, shards)
    parts = [combined] + [swap_sc(combined, h) for h in range(1, shards)]
    *blocks, slots = owner_payloads(
        ids, parts, user_power, noise_power, ap_gain, user_cluster, serving, cluster_owner,
        (aps, antennas, users, devices, shards),
    )

    pairs = lambda j: [
        (i * shards + c, (i ^ (c * per + j)) * shards + c)
        for i in range(devices)
        for c in range(shards)
    ]
    own = [lax.ppermute(blocks[j], ("ap", "sc"), pairs(j)) for j in range(per)]
    pays = own + [swap_sc(own[j], h) for h in range(1, shards) for j in range(per)]
    return owner_estimates(
        ids, slots, pays, signals, (aps, antennas, symbols, tones, devices, shards)
    )


def solution(mesh):
    placed = (
        P(("cell", "ap"), None, None, None, "sc"),
        P(("cell", "ap"), None, None, None, "sc"),
        P("cell"),
        P(("cell", "ap")),
        P(("cell", "ap"), None),
        P("cell"),
        P("cell", None),
        P("cell", None),
    )
    return jax.shard_map(
        local,
        mesh=mesh,
        in_specs=placed,
        out_specs=P(("cell", "ap"), None, None, None, "sc"),
        check_vma=False,
    )
```

```python
import functools
import math

import jax
import jax.numpy as jnp
import ml_dtypes
import numpy as np
from jax import lax
from jax.experimental import pallas as pl
from jax.experimental.pallas import tpu as pltpu
from jax.sharding import PartitionSpec as P

TONE_NUMBER = 2048
TAPS = 64
CU = 8
OWN_MAX = 4
PEER_MAX = 2
SAMPLES = 2 * TAPS
ROWS = PEER_MAX * CU
LARGE_BYTES = 58 * 1024 * 1024
VMEM_BYTES = 36 * 1024 * 1024
F32 = jnp.float32
BF16 = jnp.bfloat16


def np_parts(values, count):
    parts = []
    rest = values.astype(np.float64)
    for _ in range(count):
        part = rest.astype(np.float32).astype(ml_dtypes.bfloat16)
        parts.append(part)
        rest = rest - part.astype(np.float64)
    return parts


def np_angles(tones):
    turns = (tones[:, None] * np.arange(TAPS)[None, :]) % TONE_NUMBER
    return turns.astype(np.float64) * (2.0 * math.pi / TONE_NUMBER)


def forward_tables(shards, width):
    angles = np_angles(np.arange(shards * width))
    cosine = np.cos(angles).astype(np.float32).astype(ml_dtypes.bfloat16)
    sine = np.sin(angles).astype(np.float32).astype(ml_dtypes.bfloat16)
    real = np.concatenate([cosine, sine], axis=1).reshape(shards, width, 2 * TAPS)
    imag = np.concatenate([-sine, cosine], axis=1).reshape(shards, width, 2 * TAPS)
    return np.stack([real, imag], axis=1)


def rebuild_columns(tones):
    angles = np_angles(tones).T
    real = np.concatenate([np.cos(angles), np.sin(angles)], axis=0)
    imag = np.concatenate([-np.sin(angles), np.cos(angles)], axis=0)
    return (
        np.concatenate(np_parts(real, 2), axis=0),
        np.concatenate(np_parts(imag, 2), axis=0),
    )


def rebuild_tables(shards, width, chunk):
    real, imag = rebuild_columns(np.arange(shards * width))
    real = real.reshape(4 * TAPS, shards, width // chunk, 1, chunk)
    imag = imag.reshape(4 * TAPS, shards, width // chunk, 1, chunk)
    both = np.concatenate([real, imag], axis=3).reshape(4 * TAPS, shards, 2 * width)
    return np.ascontiguousarray(both.transpose(1, 0, 2))


def sample_table():
    real, imag = rebuild_columns(np.arange(SAMPLES) * (TONE_NUMBER // SAMPLES))
    return np.concatenate([real, imag], axis=1)


def dirichlet_tables(shards, width):
    step = TONE_NUMBER // SAMPLES
    wave = np.ones((TONE_NUMBER,), np.float64)
    tones = np.arange(TONE_NUMBER)
    for lag in range(1, TAPS):
        wave += 2.0 * np.cos(2.0 * math.pi * ((lag * tones) % TONE_NUMBER) / TONE_NUMBER)
    wave /= SAMPLES
    gap = (np.arange(shards * width)[None, :] - step * np.arange(SAMPLES)[:, None]) % TONE_NUMBER
    kernel = wave[gap]
    parts = np.concatenate(np_parts(kernel, 3), axis=0)
    parts = parts.reshape(3 * SAMPLES, shards, width)
    return np.ascontiguousarray(parts.transpose(1, 0, 2))


def three_parts(values):
    high = values.astype(BF16)
    rest = values - high.astype(F32)
    middle = rest.astype(BF16)
    low = (rest - middle.astype(F32)).astype(BF16)
    return high, middle, low


def iota(shape, axis):
    return lax.broadcasted_iota(jnp.int32, shape, axis)


def column_of(row):
    n = row.shape[1]
    return jnp.sum(jnp.where(iota((n, n), 0) == iota((n, n), 1), row, 0.0), axis=1, keepdims=True)


def row_of(column):
    n = column.shape[0]
    return jnp.sum(
        jnp.where(iota((n, n), 0) == iota((n, n), 1), column, 0.0), axis=0, keepdims=True
    )


def find_routes(shape, power, noise, gain, cluster_row, serving, owner, pick_out, weight_out, slots, extras):
    aps, antennas, users, devices, shards = shape
    per = devices // shards
    device, core = lax.axis_index("ap"), lax.axis_index("sc")
    clusters = serving.shape[0]
    extras[pl.ds(0, users), :] = jnp.broadcast_to(
        column_of(power[...]) * (1.0 / users), (users, SAMPLES)
    )
    for a in range(aps):
        extras[pl.ds(users + a, 1), :] = jnp.broadcast_to(noise[:, a : a + 1], (1, SAMPLES))

    serving_f = serving[...].astype(F32)
    columns = serving.shape[1]
    pairs = (iota((columns, devices), 0) // aps == iota((columns, devices), 1)).astype(F32)
    served = (jnp.dot(serving_f, pairs, preferred_element_type=F32) > 0.5).astype(F32)
    served_here = jnp.sum(
        jnp.where(iota((clusters, devices), 1) == device, served, 0.0), axis=1, keepdims=True
    )
    owner_row = owner[...].astype(F32)
    owner_f = column_of(owner_row)
    owner_col = owner_f.astype(jnp.int32)
    square = (clusters, clusters)
    before = iota(square, 1) < iota(square, 0)
    earlier = before & (owner_f == owner_row)
    turn = jnp.sum(jnp.where(earlier, row_of(served_here), 0.0), axis=1, keepdims=True)
    label = (owner_col ^ device) ^ (core * per)
    valid = (served_here > 0.5) & (label < per)
    base = jnp.where(valid, label.astype(F32) * ROWS + turn * CU, -4.0 * ROWS * devices)
    members = (iota((clusters, users), 0) == cluster_row[...]).astype(F32)
    prefix = (iota((users, users), 0) < iota((users, users), 1)).astype(F32)
    order = jnp.dot(members, prefix, preferred_element_type=F32)
    target = jnp.sum(members * (order + base), axis=0, keepdims=True).astype(jnp.int32)
    pick = (iota((per * ROWS, users), 0) == target).astype(F32).astype(BF16)
    pick_out[...] = pick

    weight_rows = []
    for a in range(aps):
        column = iota((clusters, columns), 1) == device * aps + a
        mine = jnp.sum(jnp.where(column, serving_f, 0.0), axis=1, keepdims=True)
        weight_rows.append(
            jnp.sum(members * mine, axis=0, keepdims=True) * gain[pl.ds(a, 1), :]
        )
    stacked = jnp.concatenate(weight_rows + [jnp.zeros((8 - aps, users), F32)], axis=0)
    weight_parts = jnp.concatenate(
        [part.astype(F32) for part in three_parts(stacked)]
        + [jnp.zeros((2 * TAPS - 24, users), F32)],
        axis=0,
    ).astype(BF16)
    weight_out[...] = lax.dot_general(
        pick, weight_parts, (((1,), (1,)), ((), ())), preferred_element_type=F32
    ).astype(BF16)

    mine = (owner_col == device).astype(F32)
    rank = jnp.sum(jnp.where(before, row_of(mine), 0.0), axis=1, keepdims=True)
    here = mine * served
    turns = jnp.dot(before.astype(F32), here, preferred_element_type=F32)
    for p in range(PEER_MAX):
        hit = jnp.where(turns == float(p), here, 0.0)
        slots[pl.ds(p, 1), :] = jnp.sum(hit * rank, axis=0, keepdims=True).astype(jnp.int32)


def coefficient_kernel(shape, *refs):
    aps, antennas, users, devices, shards = shape
    guesses, table, samples = refs[:3]
    small = refs[3:9]
    out, samples_out, pick, weights, slots, extras = refs[9:15]
    held, tables, *held_small = refs[15:23]
    held_sem, table_sem, small_sem = refs[23:]
    small_copies = [
        pltpu.make_async_copy(src, dst, small_sem.at[k])
        for k, (src, dst) in enumerate(zip(small, held_small))
    ]
    table_copy = pltpu.make_async_copy(table.at[lax.axis_index("sc")], tables, table_sem.at[0])
    sample_copy = pltpu.make_async_copy(samples, samples_out, table_sem.at[1])
    big = [
        pltpu.make_async_copy(guesses.at[a, i], held.at[a * antennas + i], held_sem.at[a * antennas + i])
        for a in range(aps)
        for i in range(antennas)
    ]
    for copy in small_copies + [table_copy] + big + [sample_copy]:
        copy.start()
    for copy in small_copies:
        copy.wait()
    find_routes(shape, *held_small, pick, weights, slots, extras)
    table_copy.wait()
    group = math.gcd(2, antennas)
    tones = held.shape[-1]
    for first in range(0, aps * antennas, group):
        for k in range(group):
            big[first + k].wait()
        real = held[pl.ds(first, group), 0].reshape(group * users, tones)
        imag = held[pl.ds(first, group), 1].reshape(group * users, tones)
        total = jnp.dot(real, tables[0], preferred_element_type=F32)
        total = total + jnp.dot(imag, tables[1], preferred_element_type=F32)
        out[pl.ds(first * users, group * users), :] = (total * (1.0 / TONE_NUMBER)).astype(BF16)
    sample_copy.wait()


def delay_coefficients(guesses, power, noise, gain, cluster, serving, owner, shape):
    aps, antennas, users, devices, shards = shape
    per = devices // shards
    tones = guesses.shape[-1]
    clusters = serving.shape[0]
    table = jnp.asarray(forward_tables(shards, tones))
    samples = jnp.asarray(sample_table())
    small = [
        power.reshape(1, users), noise.reshape(1, aps), gain, cluster.reshape(1, users), serving,
        owner.reshape(1, clusters),
    ]
    hbm = pl.BlockSpec(memory_space=pltpu.HBM)
    vmem = pl.BlockSpec(memory_space=pltpu.VMEM)
    return pl.pallas_call(
        functools.partial(coefficient_kernel, shape),
        in_specs=[hbm] * (3 + len(small)),
        out_specs=[vmem] * 6,
        out_shape=[
            jax.ShapeDtypeStruct((aps * antennas * users, 2 * TAPS), BF16),
            jax.ShapeDtypeStruct(samples.shape, BF16),
            jax.ShapeDtypeStruct((per * ROWS, users), BF16),
            jax.ShapeDtypeStruct((per * ROWS, 2 * TAPS), BF16),
            jax.ShapeDtypeStruct((PEER_MAX, devices), jnp.int32),
            jax.ShapeDtypeStruct((users + 8, SAMPLES), F32),
        ],
        scratch_shapes=[
            pltpu.VMEM((aps * antennas, 2, users, tones), BF16),
            pltpu.VMEM((2, tones, 2 * TAPS), BF16),
        ]
        + [pltpu.VMEM(x.shape, x.dtype) for x in small]
        + [
            pltpu.SemaphoreType.DMA((aps * antennas,)),
            pltpu.SemaphoreType.DMA((2,)),
            pltpu.SemaphoreType.DMA((len(small),)),
        ],
        compiler_params=pltpu.CompilerParams(vmem_limit_bytes=LARGE_BYTES),
        cost_estimate=pl.CostEstimate(
            flops=4 * guesses.size * TAPS, bytes_accessed=2 * guesses.size, transcendentals=0
        ),
        name="delay_coefficients",
    )(guesses, table, samples, *small)


def payload_kernel(shape, *refs):
    aps, antennas, users, devices, shards = shape
    per = devices // shards
    parts = refs[:shards]
    table, pick, weights, extras = refs[shards : shards + 4]
    outs = refs[shards + 4 : shards + 4 + per]
    coef, smooth, cov = refs[shards + 4 + per :]

    total = parts[0][...].astype(F32)
    for part in parts[1:]:
        total = total + part[...].astype(F32)
    coef_b = total.astype(BF16)
    coef[:, : 2 * TAPS] = coef_b
    coef[:, 2 * TAPS :] = coef_b

    smooth[...] = jnp.dot(coef[...], table[...], preferred_element_type=F32)
    for a in range(aps):
        base = a * antennas * users
        sums = {}
        for start in range(0, users, 8):
            re, im = [], []
            for i in range(antennas):
                rows = smooth[pl.ds(base + i * users + start, 8), :]
                re.append(rows[:, :SAMPLES])
                im.append(rows[:, SAMPLES:])
            weight = extras[pl.ds(start, 8), :]
            for i in range(antennas):
                sre, sim = re[i] * weight, im[i] * weight
                for j in range(i + 1):
                    value = sre * re[j] + sim * im[j]
                    sums[i, j, 0] = sums[i, j, 0] + value if start else value
                    if j < i:
                        value = sim * re[j] - sre * im[j]
                        sums[i, j, 1] = sums[i, j, 1] + value if start else value
        field = 0
        for i in range(antennas):
            for j in range(i + 1):
                for c in range(2 if j < i else 1):
                    row = jnp.sum(sums[i, j, c], axis=0, keepdims=True)
                    if i == j:
                        row = row + extras[pl.ds(users + a, 1), :]
                    cov[pl.ds(a * antennas * antennas + field, 1), :] = row
                    field += 1

    cov_parts = three_parts(cov[...])
    cov_rows = cov.shape[0]
    first = aps * antennas * ROWS
    for ai in range(aps * antennas):
        chosen = jnp.dot(
            pick[...], coef[pl.ds(ai * users, users), : 2 * TAPS], preferred_element_type=F32
        ).astype(BF16)
        for j in range(per):
            outs[j][pl.ds(ai * ROWS, ROWS), :] = chosen[j * ROWS : (j + 1) * ROWS]
    for j in range(per):
        for k in range(3):
            outs[j][pl.ds(first + k * cov_rows, cov_rows), :] = cov_parts[k]
        outs[j][pl.ds(first + 3 * cov_rows, ROWS), :] = weights[pl.ds(j * ROWS, ROWS), :]


def payload_rows(aps, antennas):
    return aps * antennas * ROWS + 3 * aps * antennas * antennas + ROWS


def owner_payloads(parts, table, pick, weights, extras, shape):
    aps, antennas, users, devices, shards = shape
    per = devices // shards
    rows = payload_rows(aps, antennas)
    operands = list(parts) + [table, pick, weights, extras]
    whole = lambda dims: pl.BlockSpec(dims, lambda g: (0,) * len(dims))
    return pl.pallas_call(
        functools.partial(payload_kernel, shape),
        grid=(1,),
        in_specs=[whole(x.shape) for x in operands],
        out_specs=[whole((rows, 2 * TAPS))] * per,
        out_shape=[jax.ShapeDtypeStruct((rows, 2 * TAPS), BF16)] * per,
        scratch_shapes=[
            pltpu.VMEM((aps * antennas * users, 4 * TAPS), BF16),
            pltpu.VMEM((aps * antennas * users, 2 * SAMPLES), F32),
            pltpu.VMEM((aps * antennas * antennas, SAMPLES), F32),
        ],
        compiler_params=pltpu.CompilerParams(vmem_limit_bytes=LARGE_BYTES),
        cost_estimate=pl.CostEstimate(
            flops=4 * aps * antennas * users * 4 * TAPS * SAMPLES,
            bytes_accessed=2 * 1024 * 1024,
            transcendentals=0,
        ),
        name="owner_payloads",
    )(*operands)


def complex_times(left, right):
    return (left[0] * right[0] - left[1] * right[1], left[0] * right[1] + left[1] * right[0])


def times_conj(left, right):
    return (left[0] * right[0] + left[1] * right[1], left[1] * right[0] - left[0] * right[1])


def minus(left, right):
    return (left[0] - right[0], left[1] - right[1])


def factorize(cov, antennas):
    factor, inverse = {}, []
    for j in range(antennas):
        pivot = cov[j, j][0]
        for k in range(j):
            pivot = pivot - (factor[j, k][0] * factor[j, k][0] + factor[j, k][1] * factor[j, k][1])
        root = lax.rsqrt(pivot)
        inverse.append(root)
        for i in range(j + 1, antennas):
            running = cov[i, j]
            for k in range(j):
                running = minus(running, times_conj(factor[i, k], factor[j, k]))
            factor[i, j] = (running[0] * root, running[1] * root)
    return factor, inverse


def substitute(factor, inverse, right):
    antennas = len(inverse)
    forward = []
    for i in range(antennas):
        running = right[i]
        for k in range(i):
            running = minus(running, complex_times(factor[i, k], forward[k]))
        forward.append((running[0] * inverse[i], running[1] * inverse[i]))
    result = [None] * antennas
    for i in range(antennas - 1, -1, -1):
        running = forward[i]
        for k in range(i + 1, antennas):
            running = minus(running, times_conj(result[k], factor[k, i]))
        result[i] = (running[0] * inverse[i], running[1] * inverse[i])
    return result


def estimate_kernel(shape, chunk, labels, first_call, last_call, slots, *refs):
    aps, antennas, symbols, tones, devices, shards = shape
    per = devices // shards
    count = len(labels)
    pays, signals = refs[:count], refs[count : 2 * count]
    refs = refs[2 * count :]
    kernel_table, rebuild_table = refs[:2]
    refs = refs[2:]
    if first_call:
        out, denominator_out = refs[:2]
        refs = refs[2:]
    else:
        acc_in, denominator_in, out = refs[:3]
        refs = refs[3:]
    (
        dirichlet, rebuild, left, cov_full, cov_tiles, sig_tiles, solved, smooth, weight,
        acc, denominator, turned, table_sem,
    ) = refs
    if first_call:
        acc, denominator = out, denominator_out
    device, core = lax.axis_index("ap"), lax.axis_index("sc")
    cov_rows = aps * antennas * antennas
    coef_rows = aps * antennas * ROWS
    blocks = tones // 128

    kernel_copy = pltpu.make_async_copy(kernel_table.at[core], dirichlet, table_sem.at[0])
    rebuild_copy = pltpu.make_async_copy(rebuild_table.at[core], rebuild, table_sem.at[1])
    kernel_copy.start()
    rebuild_copy.start()

    def cov_part(k):
        rows = [pay[pl.ds(coef_rows + k * cov_rows, cov_rows), :] for pay in pays]
        return jnp.concatenate(rows, axis=0)

    kernel_copy.wait()
    high, middle, low = cov_part(0), cov_part(1), cov_part(2)
    n = SAMPLES
    cov_full[...] = (
        jnp.dot(low, dirichlet[:n], preferred_element_type=F32)
        + jnp.dot(
            jnp.concatenate([middle, middle], axis=1), dirichlet[: 2 * n], preferred_element_type=F32
        )
        + jnp.dot(
            jnp.concatenate([high, high, high], axis=1), dirichlet[...], preferred_element_type=F32
        )
    )

    for n, pay in enumerate(pays):
        rows = pay[pl.ds(0, coef_rows), :]
        left[pl.ds(n * coef_rows, coef_rows), : 2 * TAPS] = rows
        left[pl.ds(n * coef_rows, coef_rows), 2 * TAPS :] = rows
        packed = pay[pl.ds(coef_rows + 3 * cov_rows, ROWS), :].astype(F32)
        for a in range(aps):
            value = packed[:, a : a + 1] + packed[:, 8 + a : 9 + a] + packed[:, 16 + a : 17 + a]
            weight[n, a] = jnp.broadcast_to(value, (ROWS, 128))

    if first_call:
        acc[...] = jnp.zeros_like(acc)
        denominator[...] = jnp.ones_like(denominator)
    else:
        acc[...] = acc_in[...]
        denominator[...] = denominator_in[...]

    stride = labels[1] - labels[0]

    def partner(n):
        return (labels[0] + n * stride) ^ (core * per)

    for n, label in enumerate(labels):
        place = (label ^ (core * per)) // stride
        for a in range(aps):
            for i in range(antennas):
                for c in range(2):
                    rows = signals[n][a, i, c].astype(F32)
                    first = ((a * antennas + i) * 2 + c) * symbols * blocks
                    for b in range(blocks):
                        sig_tiles[place, pl.ds(first + b, symbols, stride=blocks), :] = rows[
                            :, b * 128 : (b + 1) * 128
                        ]

    def solve(l, carry):
        for r in range(0, cov_rows, 8):
            rows = cov_full[pl.ds(pl.multiple_of(l * cov_rows + r, 8), 8), :]
            for b in range(blocks):
                cov_tiles[pl.ds(r * blocks + b, 8, stride=blocks), :] = rows[:, b * 128 : (b + 1) * 128]
        for a in range(aps):
            cov = {}
            field = a * antennas * antennas
            for i in range(antennas):
                for j in range(i + 1):
                    parts = []
                    for c in range(2 if j < i else 1):
                        parts.append(cov_tiles[pl.ds(field * blocks, blocks), :])
                        field += 1
                    cov[i, j] = parts
            factor, inverse = factorize(cov, antennas)
            for s in range(symbols):
                right = []
                for i in range(antennas):
                    tiles = [
                        (((a * antennas + i) * 2 + c) * symbols + s) * blocks for c in range(2)
                    ]
                    right.append([sig_tiles[l, pl.ds(t, blocks), :] for t in tiles])
                result = substitute(factor, inverse, right)
                for i in range(antennas):
                    for c in range(2):
                        at = ((a * antennas + i) * symbols + s) * 2 + c
                        solved[l, pl.ds(at * blocks, blocks), :] = result[i][c]
        source = partner(l) ^ device
        for p in range(PEER_MAX):
            k = slots[p, source]
            for a in range(aps):
                denominator[k] = denominator[k] + weight[l, a, pl.ds(p * CU, CU), :]
        return carry

    lax.fori_loop(0, count, solve, 0)
    rebuild_copy.wait()

    def combine(l, q):
        source = partner(l) ^ device
        for h in range(chunk // 128):
            b = q * (chunk // 128) + h
            lanes = pl.ds(pl.multiple_of(b * 128, 128), 128)
            totals = [[None] * (2 * symbols) for p in range(PEER_MAX)]
            for a in range(aps):
                for i in range(antennas):
                    base = pl.multiple_of(l * coef_rows + (a * antennas + i) * ROWS, 8)
                    link = []
                    for p in range(PEER_MAX):
                        scale = weight[l, a, pl.ds(p * CU, CU), :]
                        rows = pl.ds(base + p * CU, CU)
                        link.append(
                            (
                                smooth[rows, h * 128 : (h + 1) * 128] * scale,
                                smooth[rows, chunk + h * 128 : chunk + (h + 1) * 128] * scale,
                            )
                        )
                    for s in range(symbols):
                        at = ((a * antennas + i) * symbols + s) * 2
                        xr = solved[l, pl.ds(at * blocks + b, 1), :]
                        xi = solved[l, pl.ds((at + 1) * blocks + b, 1), :]
                        xr = jnp.broadcast_to(xr, (CU, 128))
                        xi = jnp.broadcast_to(xi, (CU, 128))
                        for p in range(PEER_MAX):
                            gr, gi = link[p]
                            er = gr * xr + gi * xi
                            ei = gr * xi - gi * xr
                            if totals[p][2 * s] is None:
                                totals[p][2 * s], totals[p][2 * s + 1] = er, ei
                            else:
                                totals[p][2 * s] += er
                                totals[p][2 * s + 1] += ei
            for p in range(PEER_MAX):
                k = slots[p, source]
                for e in range(2 * symbols):
                    acc[k, e, :, lanes] = acc[k, e, :, lanes] + totals[p][e]

    def one_chunk(q, carry):
        columns = pl.ds(pl.multiple_of(q * 2 * chunk, 128), 2 * chunk)
        smooth[...] = jnp.dot(left[...], rebuild[:, columns], preferred_element_type=F32)

        def step(l, inner):
            combine(l, q)
            return inner

        lax.fori_loop(0, count, step, 0)
        return carry

    lax.fori_loop(0, tones // chunk, one_chunk, 0)

    if not last_call:
        return

    def finish(k, carry):
        inverse = 1.0 / denominator[k]
        for b in range(blocks):
            for e in range(2 * symbols):
                value = acc[k, e, :, b * 128 : (b + 1) * 128] * inverse
                turned[pl.ds(b * CU * 2 * symbols + e, CU, stride=2 * symbols), :] = value
            for m in range(CU):
                for s in range(symbols):
                    at = ((b * CU + m) * symbols + s) * 2
                    out[k, m, s, :, b * 128 : (b + 1) * 128] = turned[pl.ds(at, 2), :]
        return carry

    lax.fori_loop(0, OWN_MAX, finish, 0)


def owner_estimates(slots, pays, signals, labels, before, last_call, shape):
    aps, antennas, symbols, tones, devices, shards = shape
    chunk = min(256, tones)
    count = len(labels)
    cov_rows = aps * antennas * antennas
    coef_rows = aps * antennas * ROWS
    blocks = tones // 128
    hbm = pl.BlockSpec(memory_space=pltpu.HBM)
    vmem = pl.BlockSpec(memory_space=pltpu.VMEM)
    smem = pl.BlockSpec(memory_space=pltpu.SMEM)
    sums = (OWN_MAX, 2 * symbols, CU, tones)
    bottom = (OWN_MAX, CU, 128)
    first_call = not before
    if last_call:
        outs = [jax.ShapeDtypeStruct((OWN_MAX, CU, symbols, 2, tones), F32)]
    else:
        outs = [jax.ShapeDtypeStruct(sums, F32), jax.ShapeDtypeStruct(bottom, F32)]
    return pl.pallas_call(
        functools.partial(estimate_kernel, shape, chunk, labels, first_call, last_call),
        in_specs=[smem] + [vmem] * (2 * count) + [hbm] * 2 + [vmem] * len(before),
        out_specs=[vmem] * len(outs),
        out_shape=outs,
        scratch_shapes=[
            pltpu.VMEM((3 * SAMPLES, tones), BF16),
            pltpu.VMEM((4 * TAPS, 2 * tones), BF16),
            pltpu.VMEM((count * coef_rows, 4 * TAPS), BF16),
            pltpu.VMEM((count * cov_rows, tones), F32),
            pltpu.VMEM((cov_rows * blocks, 128), F32),
            pltpu.VMEM((count, aps * antennas * 2 * symbols * blocks, 128), F32),
            pltpu.VMEM((count, aps * antennas * 2 * symbols * blocks, 128), F32),
            pltpu.VMEM((count * coef_rows, 2 * chunk), F32),
            pltpu.VMEM((count, aps, ROWS, 128), F32),
            pltpu.VMEM(sums, F32),
            pltpu.VMEM(bottom, F32),
            pltpu.VMEM((CU * 2 * symbols * blocks, 128), F32),
            pltpu.SemaphoreType.DMA((2,)),
        ],
        compiler_params=pltpu.CompilerParams(vmem_limit_bytes=VMEM_BYTES),
        cost_estimate=pl.CostEstimate(
            flops=4 * count * coef_rows * 4 * TAPS * tones,
            bytes_accessed=8 * 1024 * 1024,
            transcendentals=0,
        ),
        name="owner_estimates",
    )(
        slots,
        *pays,
        *signals,
        jnp.asarray(dirichlet_tables(shards, tones)),
        jnp.asarray(rebuild_tables(shards, tones, chunk)),
        *before,
    )


def local(
    unsmoothed_link_guesses,
    received,
    user_power,
    noise_power,
    ap_gain,
    user_cluster,
    serving,
    cluster_owner,
):
    aps, antennas, _, users, tones = unsmoothed_link_guesses.shape
    symbols = received.shape[3]
    devices, shards = lax.axis_size("ap"), lax.axis_size("sc")
    per = devices // shards
    def swap_ap(value, v):
        return lax.ppermute(value, "ap", [(i, i ^ v) for i in range(devices)])

    def swap_sc(value, h):
        return lax.ppermute(value, "sc", [(c, c ^ h) for c in range(shards)])

    signals = [None] * devices
    for v in range(0, devices, 2):
        signals[v] = swap_ap(received, v) if v else received
    signals[1] = swap_ap(received, 1)

    combined, samples, pick, weights, slots, extras = delay_coefficients(
        unsmoothed_link_guesses, user_power, noise_power, ap_gain, user_cluster, serving,
        cluster_owner, (aps, antennas, users, devices, shards),
    )
    parts = [combined] + [swap_sc(combined, h) for h in range(1, shards)]
    blocks = owner_payloads(
        parts, samples, pick, weights, extras, (aps, antennas, users, devices, shards)
    )

    pairs = lambda j: [
        (i * shards + c, (i ^ (c * per + j)) * shards + c)
        for i in range(devices)
        for c in range(shards)
    ]
    own = [lax.ppermute(blocks[j], ("ap", "sc"), pairs(j)) for j in range(per)]
    for v in range(2, devices, 2):
        later, _ = lax.optimization_barrier((signals[v], own[0]))
        signals[v + 1] = swap_ap(later, 1)
    pays = own + [swap_sc(own[j], h) for h in range(1, shards) for j in range(per)]
    shape = (aps, antennas, symbols, tones, devices, shards)
    even, odd = list(range(0, devices, 2)), list(range(1, devices, 2))
    sums = owner_estimates(
        slots, [pays[l] for l in even], [signals[v] for v in even], even, [], False, shape
    )
    return owner_estimates(
        slots, [pays[l] for l in odd], [signals[v] for v in odd], odd, sums, True, shape
    )[0]


def solution(mesh):
    placed = (
        P(("cell", "ap"), None, None, None, "sc"),
        P(("cell", "ap"), None, None, None, "sc"),
        P("cell"),
        P(("cell", "ap")),
        P(("cell", "ap"), None),
        P("cell"),
        P("cell", None),
        P("cell", None),
    )
    return jax.shard_map(
        local,
        mesh=mesh,
        in_specs=placed,
        out_specs=P(("cell", "ap"), None, None, None, "sc"),
        check_vma=False,
    )
```

```python
import functools
import math

import jax
import jax.numpy as jnp
import ml_dtypes
import numpy as np
from jax import lax
from jax.experimental import pallas as pl
from jax.experimental.pallas import tpu as pltpu
from jax.sharding import PartitionSpec as P

TONE_NUMBER = 2048
TAPS = 64
CU = 8
OWN_MAX = 4
PEER_MAX = 2
EARLY = (1, 4)
SAMPLES = 2 * TAPS
ROWS = PEER_MAX * CU
LARGE_BYTES = 58 * 1024 * 1024
VMEM_BYTES = 36 * 1024 * 1024
F32 = jnp.float32
BF16 = jnp.bfloat16


def np_parts(values, count):
    parts = []
    rest = values.astype(np.float64)
    for _ in range(count):
        part = rest.astype(np.float32).astype(ml_dtypes.bfloat16)
        parts.append(part)
        rest = rest - part.astype(np.float64)
    return parts


def np_angles(tones):
    turns = (tones[:, None] * np.arange(TAPS)[None, :]) % TONE_NUMBER
    return turns.astype(np.float64) * (2.0 * math.pi / TONE_NUMBER)


def forward_tables(shards, width):
    angles = np_angles(np.arange(shards * width))
    cosine = np.cos(angles).astype(np.float32).astype(ml_dtypes.bfloat16)
    sine = np.sin(angles).astype(np.float32).astype(ml_dtypes.bfloat16)
    real = np.concatenate([cosine, sine], axis=1).reshape(shards, width, 2 * TAPS)
    imag = np.concatenate([-sine, cosine], axis=1).reshape(shards, width, 2 * TAPS)
    return np.stack([real, imag], axis=1)


def rebuild_columns(tones):
    angles = np_angles(tones).T
    real = np.concatenate([np.cos(angles), np.sin(angles)], axis=0)
    imag = np.concatenate([-np.sin(angles), np.cos(angles)], axis=0)
    return (
        np.concatenate(np_parts(real, 2), axis=0),
        np.concatenate(np_parts(imag, 2), axis=0),
    )


def rebuild_tables(shards, width, chunk):
    real, imag = rebuild_columns(np.arange(shards * width))
    real = real.reshape(4 * TAPS, shards, width // chunk, 1, chunk)
    imag = imag.reshape(4 * TAPS, shards, width // chunk, 1, chunk)
    both = np.concatenate([real, imag], axis=3).reshape(4 * TAPS, shards, 2 * width)
    return np.ascontiguousarray(both.transpose(1, 0, 2))


def sample_table():
    real, imag = rebuild_columns(np.arange(SAMPLES) * (TONE_NUMBER // SAMPLES))
    return np.concatenate([real, imag], axis=1)


def dirichlet_tables(shards, width):
    step = TONE_NUMBER // SAMPLES
    wave = np.ones((TONE_NUMBER,), np.float64)
    tones = np.arange(TONE_NUMBER)
    for lag in range(1, TAPS):
        wave += 2.0 * np.cos(2.0 * math.pi * ((lag * tones) % TONE_NUMBER) / TONE_NUMBER)
    wave /= SAMPLES
    gap = (np.arange(shards * width)[None, :] - step * np.arange(SAMPLES)[:, None]) % TONE_NUMBER
    kernel = wave[gap]
    parts = np.concatenate(np_parts(kernel, 3), axis=0)
    parts = parts.reshape(3 * SAMPLES, shards, width)
    return np.ascontiguousarray(parts.transpose(1, 0, 2))


def three_parts(values):
    high = values.astype(BF16)
    rest = values - high.astype(F32)
    middle = rest.astype(BF16)
    low = (rest - middle.astype(F32)).astype(BF16)
    return high, middle, low


def iota(shape, axis):
    return lax.broadcasted_iota(jnp.int32, shape, axis)


def column_of(row):
    n = row.shape[1]
    return jnp.sum(jnp.where(iota((n, n), 0) == iota((n, n), 1), row, 0.0), axis=1, keepdims=True)


def row_of(column):
    n = column.shape[0]
    return jnp.sum(
        jnp.where(iota((n, n), 0) == iota((n, n), 1), column, 0.0), axis=0, keepdims=True
    )


def find_routes(shape, power, noise, gain, cluster_row, serving, owner, pick_out, weight_out, slots, extras):
    aps, antennas, users, devices, shards = shape
    per = devices // shards
    device, core = lax.axis_index("ap"), lax.axis_index("sc")
    clusters = serving.shape[0]
    extras[pl.ds(0, users), :] = jnp.broadcast_to(
        column_of(power[...]) * (1.0 / users), (users, SAMPLES)
    )
    for a in range(aps):
        extras[pl.ds(users + a, 1), :] = jnp.broadcast_to(noise[:, a : a + 1], (1, SAMPLES))

    serving_f = serving[...].astype(F32)
    columns = serving.shape[1]
    pairs = (iota((columns, devices), 0) // aps == iota((columns, devices), 1)).astype(F32)
    served = (jnp.dot(serving_f, pairs, preferred_element_type=F32) > 0.5).astype(F32)
    served_here = jnp.sum(
        jnp.where(iota((clusters, devices), 1) == device, served, 0.0), axis=1, keepdims=True
    )
    owner_row = owner[...].astype(F32)
    owner_f = column_of(owner_row)
    owner_col = owner_f.astype(jnp.int32)
    square = (clusters, clusters)
    before = iota(square, 1) < iota(square, 0)
    earlier = before & (owner_f == owner_row)
    turn = jnp.sum(jnp.where(earlier, row_of(served_here), 0.0), axis=1, keepdims=True)
    label = (owner_col ^ device) ^ (core * per)
    valid = (served_here > 0.5) & (label < per)
    base = jnp.where(valid, label.astype(F32) * ROWS + turn * CU, -4.0 * ROWS * devices)
    members = (iota((clusters, users), 0) == cluster_row[...]).astype(F32)
    prefix = (iota((users, users), 0) < iota((users, users), 1)).astype(F32)
    order = jnp.dot(members, prefix, preferred_element_type=F32)
    target = jnp.sum(members * (order + base), axis=0, keepdims=True).astype(jnp.int32)
    pick = (iota((per * ROWS, users), 0) == target).astype(F32).astype(BF16)
    pick_out[...] = pick

    weight_rows = []
    for a in range(aps):
        column = iota((clusters, columns), 1) == device * aps + a
        mine = jnp.sum(jnp.where(column, serving_f, 0.0), axis=1, keepdims=True)
        weight_rows.append(
            jnp.sum(members * mine, axis=0, keepdims=True) * gain[pl.ds(a, 1), :]
        )
    stacked = jnp.concatenate(weight_rows + [jnp.zeros((8 - aps, users), F32)], axis=0)
    weight_parts = jnp.concatenate(
        [part.astype(F32) for part in three_parts(stacked)]
        + [jnp.zeros((2 * TAPS - 24, users), F32)],
        axis=0,
    ).astype(BF16)
    weight_out[...] = lax.dot_general(
        pick, weight_parts, (((1,), (1,)), ((), ())), preferred_element_type=F32
    ).astype(BF16)

    mine = (owner_col == device).astype(F32)
    rank = jnp.sum(jnp.where(before, row_of(mine), 0.0), axis=1, keepdims=True)
    here = mine * served
    turns = jnp.dot(before.astype(F32), here, preferred_element_type=F32)
    for p in range(PEER_MAX):
        hit = jnp.where(turns == float(p), here, 0.0)
        slots[pl.ds(p, 1), :] = jnp.sum(hit * rank, axis=0, keepdims=True).astype(jnp.int32)


def coefficient_kernel(shape, *refs):
    aps, antennas, users, devices, shards = shape
    guesses, table, samples = refs[:3]
    small = refs[3:9]
    out, samples_out, pick, weights, slots, extras = refs[9:15]
    held, tables, *held_small = refs[15:23]
    held_sem, table_sem, small_sem = refs[23:]
    small_copies = [
        pltpu.make_async_copy(src, dst, small_sem.at[k])
        for k, (src, dst) in enumerate(zip(small, held_small))
    ]
    table_copy = pltpu.make_async_copy(table.at[lax.axis_index("sc")], tables, table_sem.at[0])
    sample_copy = pltpu.make_async_copy(samples, samples_out, table_sem.at[1])
    big = [
        pltpu.make_async_copy(guesses.at[a, i], held.at[a * antennas + i], held_sem.at[a * antennas + i])
        for a in range(aps)
        for i in range(antennas)
    ]
    for copy in small_copies + [table_copy] + big + [sample_copy]:
        copy.start()
    for copy in small_copies:
        copy.wait()
    find_routes(shape, *held_small, pick, weights, slots, extras)
    table_copy.wait()
    group = math.gcd(2, antennas)
    tones = held.shape[-1]
    for first in range(0, aps * antennas, group):
        for k in range(group):
            big[first + k].wait()
        real = held[pl.ds(first, group), 0].reshape(group * users, tones)
        imag = held[pl.ds(first, group), 1].reshape(group * users, tones)
        total = jnp.dot(real, tables[0], preferred_element_type=F32)
        total = total + jnp.dot(imag, tables[1], preferred_element_type=F32)
        out[pl.ds(first * users, group * users), :] = (total * (1.0 / TONE_NUMBER)).astype(BF16)
    sample_copy.wait()


def delay_coefficients(guesses, power, noise, gain, cluster, serving, owner, shape):
    aps, antennas, users, devices, shards = shape
    per = devices // shards
    tones = guesses.shape[-1]
    clusters = serving.shape[0]
    table = jnp.asarray(forward_tables(shards, tones))
    samples = jnp.asarray(sample_table())
    small = [
        power.reshape(1, users), noise.reshape(1, aps), gain, cluster.reshape(1, users), serving,
        owner.reshape(1, clusters),
    ]
    hbm = pl.BlockSpec(memory_space=pltpu.HBM)
    vmem = pl.BlockSpec(memory_space=pltpu.VMEM)
    return pl.pallas_call(
        functools.partial(coefficient_kernel, shape),
        in_specs=[hbm] * (3 + len(small)),
        out_specs=[vmem] * 6,
        out_shape=[
            jax.ShapeDtypeStruct((aps * antennas * users, 2 * TAPS), BF16),
            jax.ShapeDtypeStruct(samples.shape, BF16),
            jax.ShapeDtypeStruct((per * ROWS, users), BF16),
            jax.ShapeDtypeStruct((per * ROWS, 2 * TAPS), BF16),
            jax.ShapeDtypeStruct((PEER_MAX, devices), jnp.int32),
            jax.ShapeDtypeStruct((users + 8, SAMPLES), F32),
        ],
        scratch_shapes=[
            pltpu.VMEM((aps * antennas, 2, users, tones), BF16),
            pltpu.VMEM((2, tones, 2 * TAPS), BF16),
        ]
        + [pltpu.VMEM(x.shape, x.dtype) for x in small]
        + [
            pltpu.SemaphoreType.DMA((aps * antennas,)),
            pltpu.SemaphoreType.DMA((2,)),
            pltpu.SemaphoreType.DMA((len(small),)),
        ],
        compiler_params=pltpu.CompilerParams(vmem_limit_bytes=LARGE_BYTES),
        cost_estimate=pl.CostEstimate(
            flops=4 * guesses.size * TAPS, bytes_accessed=2 * guesses.size, transcendentals=0
        ),
        name="delay_coefficients",
    )(guesses, table, samples, *small)


def payload_kernel(shape, *refs):
    aps, antennas, users, devices, shards = shape
    per = devices // shards
    parts = refs[:shards]
    table, pick, weights, extras = refs[shards : shards + 4]
    outs = refs[shards + 4 : shards + 4 + per]
    coef, smooth, cov = refs[shards + 4 + per :]

    total = parts[0][...].astype(F32)
    for part in parts[1:]:
        total = total + part[...].astype(F32)
    coef_b = total.astype(BF16)
    coef[:, : 2 * TAPS] = coef_b
    coef[:, 2 * TAPS :] = coef_b

    smooth[...] = jnp.dot(coef[...], table[...], preferred_element_type=F32)
    for a in range(aps):
        base = a * antennas * users
        sums = {}
        for start in range(0, users, 8):
            re, im = [], []
            for i in range(antennas):
                rows = smooth[pl.ds(base + i * users + start, 8), :]
                re.append(rows[:, :SAMPLES])
                im.append(rows[:, SAMPLES:])
            weight = extras[pl.ds(start, 8), :]
            for i in range(antennas):
                sre, sim = re[i] * weight, im[i] * weight
                for j in range(i + 1):
                    value = sre * re[j] + sim * im[j]
                    sums[i, j, 0] = sums[i, j, 0] + value if start else value
                    if j < i:
                        value = sim * re[j] - sre * im[j]
                        sums[i, j, 1] = sums[i, j, 1] + value if start else value
        field = 0
        for i in range(antennas):
            for j in range(i + 1):
                for c in range(2 if j < i else 1):
                    row = jnp.sum(sums[i, j, c], axis=0, keepdims=True)
                    if i == j:
                        row = row + extras[pl.ds(users + a, 1), :]
                    cov[pl.ds(a * antennas * antennas + field, 1), :] = row
                    field += 1

    cov_parts = three_parts(cov[...])
    cov_rows = cov.shape[0]
    first = aps * antennas * ROWS
    for ai in range(aps * antennas):
        chosen = jnp.dot(
            pick[...], coef[pl.ds(ai * users, users), : 2 * TAPS], preferred_element_type=F32
        ).astype(BF16)
        for j in range(per):
            outs[j][pl.ds(ai * ROWS, ROWS), :] = chosen[j * ROWS : (j + 1) * ROWS]
    for j in range(per):
        for k in range(3):
            outs[j][pl.ds(first + k * cov_rows, cov_rows), :] = cov_parts[k]
        outs[j][pl.ds(first + 3 * cov_rows, ROWS), :] = weights[pl.ds(j * ROWS, ROWS), :]


def payload_rows(aps, antennas):
    return aps * antennas * ROWS + 3 * aps * antennas * antennas + ROWS


def owner_payloads(parts, table, pick, weights, extras, shape):
    aps, antennas, users, devices, shards = shape
    per = devices // shards
    rows = payload_rows(aps, antennas)
    operands = list(parts) + [table, pick, weights, extras]
    whole = lambda dims: pl.BlockSpec(dims, lambda g: (0,) * len(dims))
    return pl.pallas_call(
        functools.partial(payload_kernel, shape),
        grid=(1,),
        in_specs=[whole(x.shape) for x in operands],
        out_specs=[whole((rows, 2 * TAPS))] * per,
        out_shape=[jax.ShapeDtypeStruct((rows, 2 * TAPS), BF16)] * per,
        scratch_shapes=[
            pltpu.VMEM((aps * antennas * users, 4 * TAPS), BF16),
            pltpu.VMEM((aps * antennas * users, 2 * SAMPLES), F32),
            pltpu.VMEM((aps * antennas * antennas, SAMPLES), F32),
        ],
        compiler_params=pltpu.CompilerParams(vmem_limit_bytes=LARGE_BYTES),
        cost_estimate=pl.CostEstimate(
            flops=4 * aps * antennas * users * 4 * TAPS * SAMPLES,
            bytes_accessed=2 * 1024 * 1024,
            transcendentals=0,
        ),
        name="owner_payloads",
    )(*operands)


def complex_times(left, right):
    return (left[0] * right[0] - left[1] * right[1], left[0] * right[1] + left[1] * right[0])


def times_conj(left, right):
    return (left[0] * right[0] + left[1] * right[1], left[1] * right[0] - left[0] * right[1])


def minus(left, right):
    return (left[0] - right[0], left[1] - right[1])


def factorize(cov, antennas):
    factor, inverse = {}, []
    for j in range(antennas):
        pivot = cov[j, j][0]
        for k in range(j):
            pivot = pivot - (factor[j, k][0] * factor[j, k][0] + factor[j, k][1] * factor[j, k][1])
        root = lax.rsqrt(pivot)
        inverse.append(root)
        for i in range(j + 1, antennas):
            running = cov[i, j]
            for k in range(j):
                running = minus(running, times_conj(factor[i, k], factor[j, k]))
            factor[i, j] = (running[0] * root, running[1] * root)
    return factor, inverse


def substitute(factor, inverse, right):
    antennas = len(inverse)
    forward = []
    for i in range(antennas):
        running = right[i]
        for k in range(i):
            running = minus(running, complex_times(factor[i, k], forward[k]))
        forward.append((running[0] * inverse[i], running[1] * inverse[i]))
    result = [None] * antennas
    for i in range(antennas - 1, -1, -1):
        running = forward[i]
        for k in range(i + 1, antennas):
            running = minus(running, times_conj(result[k], factor[k, i]))
        result[i] = (running[0] * inverse[i], running[1] * inverse[i])
    return result


def estimate_kernel(shape, chunk, group, slots, *refs):
    aps, antennas, symbols, tones, devices, shards = shape
    count = devices // shards
    first_call, last_call = group == 0, group == shards - 1
    pays, signals = refs[:devices], refs[devices : devices + count]
    refs = refs[devices + count :]
    kernel_table, rebuild_table = refs[:2]
    refs = refs[2:]
    if first_call:
        out, denominator_out = refs[:2]
        refs = refs[2:]
    else:
        acc_in, denominator_in, out = refs[:3]
        refs = refs[3:]
    (
        left, cov_full, cov_tiles, sig_tiles, solved, smooth, weight,
        acc, denominator, turned, staged, out_sem,
    ) = refs
    if first_call:
        acc, denominator = out, denominator_out
    device, core = lax.axis_index("ap"), lax.axis_index("sc")
    cov_rows = aps * antennas * antennas
    coef_rows = aps * antennas * ROWS
    blocks = tones // 128

    dirichlet, rebuild = kernel_table.at[core], rebuild_table.at[core]

    def payload(n, start, size):
        value = pays[n][pl.ds(start, size), :]
        for h in range(1, shards):
            value = jnp.where(
                (core ^ h) == group, pays[h * count + n][pl.ds(start, size), :], value
            )
        return value

    def cov_part(k):
        return jnp.concatenate(
            [payload(n, coef_rows + k * cov_rows, cov_rows) for n in range(count)], axis=0
        )

    high, middle, low = cov_part(0), cov_part(1), cov_part(2)
    n = SAMPLES
    cov_full[...] = (
        jnp.dot(low, dirichlet[:n], preferred_element_type=F32)
        + jnp.dot(
            jnp.concatenate([middle, middle], axis=1), dirichlet[: 2 * n], preferred_element_type=F32
        )
        + jnp.dot(
            jnp.concatenate([high, high, high], axis=1), dirichlet[...], preferred_element_type=F32
        )
    )

    for n in range(count):
        rows = payload(n, 0, coef_rows)
        left[pl.ds(n * coef_rows, coef_rows), : 2 * TAPS] = rows
        left[pl.ds(n * coef_rows, coef_rows), 2 * TAPS :] = rows
        packed = payload(n, coef_rows + 3 * cov_rows, ROWS).astype(F32)
        for a in range(aps):
            value = packed[:, a : a + 1] + packed[:, 8 + a : 9 + a] + packed[:, 16 + a : 17 + a]
            weight[n, a] = jnp.broadcast_to(value, (ROWS, 128))

    if first_call:
        acc[...] = jnp.zeros_like(acc)
        denominator[...] = jnp.ones_like(denominator)
    else:
        acc[...] = acc_in[...]
        denominator[...] = denominator_in[...]

    for n in range(count):
        for a in range(aps):
            for i in range(antennas):
                for c in range(2):
                    rows = signals[n][a, i, c].astype(F32)
                    first = ((a * antennas + i) * 2 + c) * symbols * blocks
                    for b in range(blocks):
                        sig_tiles[n, pl.ds(first + b, symbols, stride=blocks), :] = rows[
                            :, b * 128 : (b + 1) * 128
                        ]

    def solve(l, carry):
        for r in range(0, cov_rows, 8):
            rows = cov_full[pl.ds(pl.multiple_of(l * cov_rows + r, 8), 8), :]
            for b in range(blocks):
                cov_tiles[pl.ds(r * blocks + b, 8, stride=blocks), :] = rows[:, b * 128 : (b + 1) * 128]
        for a in range(aps):
            cov = {}
            field = a * antennas * antennas
            for i in range(antennas):
                for j in range(i + 1):
                    parts = []
                    for c in range(2 if j < i else 1):
                        parts.append(cov_tiles[pl.ds(field * blocks, blocks), :])
                        field += 1
                    cov[i, j] = parts
            factor, inverse = factorize(cov, antennas)
            for s in range(symbols):
                right = []
                for i in range(antennas):
                    tiles = [
                        (((a * antennas + i) * 2 + c) * symbols + s) * blocks for c in range(2)
                    ]
                    right.append([sig_tiles[l, pl.ds(t, blocks), :] for t in tiles])
                result = substitute(factor, inverse, right)
                for i in range(antennas):
                    re, im = result[i]
                    at = ((a * antennas + i) * symbols + s) * 3
                    for c, tile in enumerate((re, im - re, re + im)):
                        solved[l, pl.ds((at + c) * blocks, blocks), :] = tile
        source = (group * count + l) ^ device
        for p in range(PEER_MAX):
            k = slots[p, source]
            for a in range(aps):
                denominator[k] = denominator[k] + weight[l, a, pl.ds(p * CU, CU), :]
        return carry

    lax.fori_loop(0, count, solve, 0)

    def combine(l, q):
        source = (group * count + l) ^ device
        for h in range(chunk // 128):
            b = q * (chunk // 128) + h
            lanes = pl.ds(pl.multiple_of(b * 128, 128), 128)
            totals = [[None] * (3 * symbols) for p in range(PEER_MAX)]
            for a in range(aps):
                for i in range(antennas):
                    base = pl.multiple_of(l * coef_rows + (a * antennas + i) * ROWS, 8)
                    link = []
                    for p in range(PEER_MAX):
                        scale = weight[l, a, pl.ds(p * CU, CU), :]
                        rows = pl.ds(base + p * CU, CU)
                        re = smooth[rows, h * 128 : (h + 1) * 128] * scale
                        im = smooth[rows, chunk + h * 128 : chunk + (h + 1) * 128] * scale
                        link.append((re - im, re, im))
                    for s in range(symbols):
                        at = ((a * antennas + i) * symbols + s) * 3
                        for c in range(3):
                            x = solved[l, pl.ds((at + c) * blocks + b, 1), :]
                            x = jnp.broadcast_to(x, (CU, 128))
                            for p in range(PEER_MAX):
                                value = link[p][c] * x
                                old = totals[p][3 * s + c]
                                totals[p][3 * s + c] = value if old is None else old + value
            for p in range(PEER_MAX):
                k = slots[p, source]
                for s in range(symbols):
                    both, upper, lower = totals[p][3 * s : 3 * s + 3]
                    acc[k, 2 * s, :, lanes] = acc[k, 2 * s, :, lanes] + (both + lower)
                    acc[k, 2 * s + 1, :, lanes] = acc[k, 2 * s + 1, :, lanes] + (both + upper)

    chunks = tones // chunk

    def output_copy(q):
        lanes = pl.ds(pl.multiple_of(q * chunk, 128), chunk)
        return pltpu.make_async_copy(staged.at[q], out.at[:, :, :, :, lanes], out_sem.at[q])

    def finish(q):
        for k in range(OWN_MAX):
            inverse = 1.0 / denominator[k]
            first = k * CU * 2 * symbols
            for h in range(chunk // 128):
                lanes = pl.ds(pl.multiple_of(q * chunk + h * 128, 128), 128)
                for e in range(2 * symbols):
                    value = acc[k, e, :, lanes] * inverse
                    turned[pl.ds(first + e, CU, stride=2 * symbols), :] = value
                for m in range(CU):
                    for s in range(symbols):
                        at = first + (m * symbols + s) * 2
                        staged[q, k, m, s, :, h * 128 : (h + 1) * 128] = turned[pl.ds(at, 2), :]
        output_copy(q).start()

    def one_chunk(q, carry):
        columns = pl.ds(pl.multiple_of(q * 2 * chunk, 128), 2 * chunk)
        smooth[...] = jnp.dot(left[...], rebuild[:, columns], preferred_element_type=F32)

        def step(l, inner):
            combine(l, q)
            return inner

        lax.fori_loop(0, count, step, 0)
        if last_call:
            finish(q)
        return carry

    lax.fori_loop(0, chunks, one_chunk, 0)
    if last_call:
        for q in range(chunks):
            output_copy(q).wait()


def owner_estimates(slots, pays, signals, group, before, shape):
    aps, antennas, symbols, tones, devices, shards = shape
    chunk = min(512, tones // 2)
    count = devices // shards
    last_call = group == shards - 1
    cov_rows = aps * antennas * antennas
    coef_rows = aps * antennas * ROWS
    blocks = tones // 128
    hbm = pl.BlockSpec(memory_space=pltpu.HBM)
    vmem = pl.BlockSpec(memory_space=pltpu.VMEM)
    smem = pl.BlockSpec(memory_space=pltpu.SMEM)
    sums = (OWN_MAX, 2 * symbols, CU, tones)
    bottom = (OWN_MAX, CU, 128)
    if last_call:
        outs = [jax.ShapeDtypeStruct((OWN_MAX, CU, symbols, 2, tones), F32)]
    else:
        outs = [jax.ShapeDtypeStruct(sums, F32), jax.ShapeDtypeStruct(bottom, F32)]
    return pl.pallas_call(
        functools.partial(estimate_kernel, shape, chunk, group),
        in_specs=[smem] + [vmem] * (len(pays) + len(signals) + 2 + len(before)),
        out_specs=[hbm] if last_call else [vmem] * len(outs),
        out_shape=outs,
        scratch_shapes=[
            pltpu.VMEM((count * coef_rows, 4 * TAPS), BF16),
            pltpu.VMEM((count * cov_rows, tones), F32),
            pltpu.VMEM((cov_rows * blocks, 128), F32),
            pltpu.VMEM((count, aps * antennas * 2 * symbols * blocks, 128), F32),
            pltpu.VMEM((count, aps * antennas * 3 * symbols * blocks, 128), F32),
            pltpu.VMEM((count * coef_rows, 2 * chunk), F32),
            pltpu.VMEM((count, aps, ROWS, 128), F32),
            pltpu.VMEM(sums, F32),
            pltpu.VMEM(bottom, F32),
            pltpu.VMEM((CU * 2 * symbols * OWN_MAX, 128), F32),
            pltpu.VMEM((tones // chunk, OWN_MAX, CU, symbols, 2, chunk), F32),
            pltpu.SemaphoreType.DMA((tones // chunk,)),
        ],
        compiler_params=pltpu.CompilerParams(vmem_limit_bytes=VMEM_BYTES),
        cost_estimate=pl.CostEstimate(
            flops=4 * count * coef_rows * 4 * TAPS * tones,
            bytes_accessed=8 * 1024 * 1024,
            transcendentals=0,
        ),
        name="owner_estimates",
    )(
        slots,
        *pays,
        *signals,
        jnp.asarray(dirichlet_tables(shards, tones)),
        jnp.asarray(rebuild_tables(shards, tones, chunk)),
        *before,
    )


def local(
    unsmoothed_link_guesses,
    received,
    user_power,
    noise_power,
    ap_gain,
    user_cluster,
    serving,
    cluster_owner,
):
    aps, antennas, _, users, tones = unsmoothed_link_guesses.shape
    symbols = received.shape[3]
    devices, shards = lax.axis_size("ap"), lax.axis_size("sc")
    per = devices // shards
    def swap_ap(value, v):
        return lax.ppermute(value, "ap", [(i, i ^ v) for i in range(devices)])

    def swap_sc(value, h):
        return lax.ppermute(value, "sc", [(c, c ^ h) for c in range(shards)])

    signals = [None] * devices
    for v in range(0, devices, 2):
        signals[v] = swap_ap(received, v) if v else received
    signals[1] = swap_ap(received, 1)

    combined, samples, pick, weights, slots, extras = delay_coefficients(
        unsmoothed_link_guesses, user_power, noise_power, ap_gain, user_cluster, serving,
        cluster_owner, (aps, antennas, users, devices, shards),
    )
    combined, early = lax.optimization_barrier((combined, [signals[v] for v in EARLY]))
    for v, value in zip(EARLY, early):
        signals[v] = value
    parts = [combined] + [swap_sc(combined, h) for h in range(1, shards)]
    blocks = owner_payloads(
        parts, samples, pick, weights, extras, (aps, antennas, users, devices, shards)
    )

    pairs = lambda j: [
        (i * shards + c, (i ^ (c * per + j)) * shards + c)
        for i in range(devices)
        for c in range(shards)
    ]
    own = [lax.ppermute(blocks[j], ("ap", "sc"), pairs(j)) for j in range(per)]
    pays = own + [swap_sc(own[j], h) for h in range(1, shards) for j in range(per)]
    for v in range(2, devices, 2):
        value = signals[v] if v in EARLY else lax.optimization_barrier((signals[v], own[0]))[0]
        signals[v + 1] = swap_ap(value, 1)
    shape = (aps, antennas, symbols, tones, devices, shards)
    result = []
    for group in range(shards):
        result = owner_estimates(
            slots, pays, signals[group * per : (group + 1) * per], group, result, shape
        )
    return result[0]


def solution(mesh):
    placed = (
        P(("cell", "ap"), None, None, None, "sc"),
        P(("cell", "ap"), None, None, None, "sc"),
        P("cell"),
        P(("cell", "ap")),
        P(("cell", "ap"), None),
        P("cell"),
        P("cell", None),
        P("cell", None),
    )
    return jax.shard_map(
        local,
        mesh=mesh,
        in_specs=placed,
        out_specs=P(("cell", "ap"), None, None, None, "sc"),
        check_vma=False,
    )
```

```python
import functools
import math

import jax
import jax.numpy as jnp
import ml_dtypes
import numpy as np
from jax import lax
from jax.experimental import pallas as pl
from jax.experimental.pallas import tpu as pltpu
from jax.sharding import PartitionSpec as P

TONE_NUMBER = 2048
TAPS = 64
CU = 8
OWN_MAX = 4
PEER_MAX = 2
EARLY = (1, 4)
SAMPLES = 2 * TAPS
ROWS = PEER_MAX * CU
LARGE_BYTES = 52 * 1024 * 1024
SMALL_BYTES = 24 * 1024 * 1024
TABLE_ROWS = 32 * 1024
VMEM_BYTES = 36 * 1024 * 1024
F32 = jnp.float32
BF16 = jnp.bfloat16


def np_parts(values, count):
    parts = []
    rest = values.astype(np.float64)
    for _ in range(count):
        part = rest.astype(np.float32).astype(ml_dtypes.bfloat16)
        parts.append(part)
        rest = rest - part.astype(np.float64)
    return parts


def np_angles(tones):
    turns = (tones[:, None] * np.arange(TAPS)[None, :]) % TONE_NUMBER
    return turns.astype(np.float64) * (2.0 * math.pi / TONE_NUMBER)


def forward_tables(shards, width):
    angles = np_angles(np.arange(shards * width))
    cosine = np.cos(angles).astype(np.float32).astype(ml_dtypes.bfloat16)
    sine = np.sin(angles).astype(np.float32).astype(ml_dtypes.bfloat16)
    real = np.concatenate([cosine, sine], axis=1).reshape(shards, width, 2 * TAPS)
    imag = np.concatenate([-sine, cosine], axis=1).reshape(shards, width, 2 * TAPS)
    return np.stack([real, imag], axis=1)


def rebuild_columns(tones):
    angles = np_angles(tones).T
    real = np.concatenate([np.cos(angles), np.sin(angles)], axis=0)
    imag = np.concatenate([-np.sin(angles), np.cos(angles)], axis=0)
    return (
        np.concatenate(np_parts(real, 2), axis=0),
        np.concatenate(np_parts(imag, 2), axis=0),
    )


def rebuild_tables(shards, width, chunk):
    real, imag = rebuild_columns(np.arange(shards * width))
    real = real.reshape(4 * TAPS, shards, width // chunk, 1, chunk)
    imag = imag.reshape(4 * TAPS, shards, width // chunk, 1, chunk)
    both = np.concatenate([real, imag], axis=3).reshape(4 * TAPS, shards, 2 * width)
    return np.ascontiguousarray(both.transpose(1, 0, 2))


def sample_table():
    real, imag = rebuild_columns(np.arange(SAMPLES) * (TONE_NUMBER // SAMPLES))
    return np.concatenate([real, imag], axis=1)


def first_tables(shards, width):
    forward = forward_tables(shards, width).reshape(shards * 2 * width, 2 * TAPS)
    samples = sample_table()
    rows = np.concatenate([forward, samples[:, :SAMPLES], samples[:, SAMPLES:]], axis=0)
    filling = max(0, TABLE_ROWS - rows.shape[0])
    return np.concatenate([rows, np.zeros((filling, 2 * TAPS), ml_dtypes.bfloat16)], axis=0)


def dirichlet_tables(shards, width):
    step = TONE_NUMBER // SAMPLES
    wave = np.ones((TONE_NUMBER,), np.float64)
    tones = np.arange(TONE_NUMBER)
    for lag in range(1, TAPS):
        wave += 2.0 * np.cos(2.0 * math.pi * ((lag * tones) % TONE_NUMBER) / TONE_NUMBER)
    wave /= SAMPLES
    gap = (np.arange(shards * width)[None, :] - step * np.arange(SAMPLES)[:, None]) % TONE_NUMBER
    kernel = wave[gap]
    parts = np.concatenate(np_parts(kernel, 3), axis=0)
    parts = parts.reshape(3 * SAMPLES, shards, width)
    return np.ascontiguousarray(parts.transpose(1, 0, 2))


def three_parts(values):
    high = values.astype(BF16)
    rest = values - high.astype(F32)
    middle = rest.astype(BF16)
    low = (rest - middle.astype(F32)).astype(BF16)
    return high, middle, low


def iota(shape, axis):
    return lax.broadcasted_iota(jnp.int32, shape, axis)


def column_of(row):
    n = row.shape[1]
    return jnp.sum(jnp.where(iota((n, n), 0) == iota((n, n), 1), row, 0.0), axis=1, keepdims=True)


def row_of(column):
    n = column.shape[0]
    return jnp.sum(
        jnp.where(iota((n, n), 0) == iota((n, n), 1), column, 0.0), axis=0, keepdims=True
    )


def pack_rows(power, noise, gain, cluster, serving, owner):
    width = max(power.shape[0], serving.shape[1], serving.shape[0])
    rows = [
        power[None, :], gain, cluster.astype(F32)[None, :], serving.astype(F32),
        owner.astype(F32).reshape(1, -1), noise[None, :],
    ]
    return jnp.concatenate([jnp.pad(x, ((0, 0), (0, width - x.shape[1]))) for x in rows], axis=0)


def find_routes(shape, clusters, packed, pick_out, weight_out, slots, extras):
    aps, antennas, users, devices, shards = shape
    per = devices // shards
    device, core = lax.axis_index("ap"), lax.axis_index("sc")
    power = packed[pl.ds(0, 1), :][:, :users]
    gain = [packed[pl.ds(1 + a, 1), :][:, :users] for a in range(aps)]
    cluster_row = packed[pl.ds(1 + aps, 1), :][:, :users]
    serving_f = packed[pl.ds(2 + aps, clusters), :][:, : aps * devices]
    owner_row = packed[pl.ds(2 + aps + clusters, 1), :][:, :clusters]
    noise = packed[pl.ds(3 + aps + clusters, 1), :]
    extras[pl.ds(0, users), :] = jnp.broadcast_to(
        column_of(power) * (1.0 / users), (users, SAMPLES)
    )
    for a in range(aps):
        extras[pl.ds(users + a, 1), :] = jnp.broadcast_to(noise[:, a : a + 1], (1, SAMPLES))

    columns = aps * devices
    pairs = (iota((columns, devices), 0) // aps == iota((columns, devices), 1)).astype(F32)
    served = (jnp.dot(serving_f, pairs, preferred_element_type=F32) > 0.5).astype(F32)
    served_here = jnp.sum(
        jnp.where(iota((clusters, devices), 1) == device, served, 0.0), axis=1, keepdims=True
    )
    owner_f = column_of(owner_row)
    owner_col = owner_f.astype(jnp.int32)
    square = (clusters, clusters)
    before = iota(square, 1) < iota(square, 0)
    earlier = before & (owner_f == owner_row)
    turn = jnp.sum(jnp.where(earlier, row_of(served_here), 0.0), axis=1, keepdims=True)
    label = (owner_col ^ device) ^ (core * per)
    valid = (served_here > 0.5) & (label < per)
    base = jnp.where(valid, label.astype(F32) * ROWS + turn * CU, -4.0 * ROWS * devices)
    members = (iota((clusters, users), 0).astype(F32) == cluster_row).astype(F32)
    prefix = (iota((users, users), 0) < iota((users, users), 1)).astype(F32)
    order = jnp.dot(members, prefix, preferred_element_type=F32)
    target = jnp.sum(members * (order + base), axis=0, keepdims=True).astype(jnp.int32)
    pick = (iota((per * ROWS, users), 0) == target).astype(F32).astype(BF16)
    pick_out[...] = pick

    weight_rows = []
    for a in range(aps):
        column = iota((clusters, columns), 1) == device * aps + a
        mine = jnp.sum(jnp.where(column, serving_f, 0.0), axis=1, keepdims=True)
        weight_rows.append(
            jnp.sum(members * mine, axis=0, keepdims=True) * gain[a]
        )
    stacked = jnp.concatenate(weight_rows + [jnp.zeros((8 - aps, users), F32)], axis=0)
    weight_parts = jnp.concatenate(
        [part.astype(F32) for part in three_parts(stacked)]
        + [jnp.zeros((2 * TAPS - 24, users), F32)],
        axis=0,
    ).astype(BF16)
    weight_out[...] = lax.dot_general(
        pick, weight_parts, (((1,), (1,)), ((), ())), preferred_element_type=F32
    ).astype(BF16)

    mine = (owner_col == device).astype(F32)
    rank = jnp.sum(jnp.where(before, row_of(mine), 0.0), axis=1, keepdims=True)
    here = mine * served
    turns = jnp.dot(before.astype(F32), here, preferred_element_type=F32)
    for p in range(PEER_MAX):
        hit = jnp.where(turns == float(p), here, 0.0)
        slots[pl.ds(p, 1), :] = jnp.sum(hit * rank, axis=0, keepdims=True).astype(jnp.int32)


def coefficient_kernel(shape, clusters, *refs):
    aps, antennas, users, devices, shards = shape
    guesses, table, packed = refs[:3]
    out, samples, pick, weights, slots, extras = refs[3:9]
    held, tables, held_sem, table_sem = refs[9:]
    tones = held.shape[-1]
    first = pl.multiple_of(lax.axis_index("sc") * 2 * tones, 16)
    table_copy = pltpu.make_async_copy(table.at[pl.ds(first, 2 * tones)], tables, table_sem.at[0])
    sample_copies = [
        pltpu.make_async_copy(
            table.at[pl.ds(shards * 2 * tones + c * 4 * TAPS, 4 * TAPS)],
            samples.at[:, pl.ds(c * SAMPLES, SAMPLES)],
            table_sem.at[1 + c],
        )
        for c in range(2)
    ]
    big = [
        pltpu.make_async_copy(guesses.at[a, i], held.at[a * antennas + i], held_sem.at[a * antennas + i])
        for a in range(aps)
        for i in range(antennas)
    ]
    for copy in [table_copy] + big + sample_copies:
        copy.start()
    find_routes(shape, clusters, packed, pick, weights, slots, extras)
    table_copy.wait()
    group = math.gcd(2, antennas)
    for first in range(0, aps * antennas, group):
        for k in range(group):
            big[first + k].wait()
        real = held[pl.ds(first, group), 0].reshape(group * users, tones)
        imag = held[pl.ds(first, group), 1].reshape(group * users, tones)
        total = jnp.dot(real, tables[pl.ds(0, tones), :], preferred_element_type=F32)
        total = total + jnp.dot(imag, tables[pl.ds(tones, tones), :], preferred_element_type=F32)
        out[pl.ds(first * users, group * users), :] = (total * (1.0 / TONE_NUMBER)).astype(BF16)
    for copy in sample_copies:
        copy.wait()


def delay_coefficients(guesses, power, noise, gain, cluster, serving, owner, shape):
    aps, antennas, users, devices, shards = shape
    per = devices // shards
    tones = guesses.shape[-1]
    clusters = serving.shape[0]
    table = jnp.asarray(first_tables(shards, tones))
    packed = pack_rows(power, noise, gain, cluster, serving, owner)
    hbm = pl.BlockSpec(memory_space=pltpu.HBM)
    vmem = pl.BlockSpec(memory_space=pltpu.VMEM)
    return pl.pallas_call(
        functools.partial(coefficient_kernel, shape, clusters),
        in_specs=[hbm, hbm, vmem],
        out_specs=[vmem] * 6,
        out_shape=[
            jax.ShapeDtypeStruct((aps * antennas * users, 2 * TAPS), BF16),
            jax.ShapeDtypeStruct((4 * TAPS, 2 * SAMPLES), BF16),
            jax.ShapeDtypeStruct((per * ROWS, users), BF16),
            jax.ShapeDtypeStruct((per * ROWS, 2 * TAPS), BF16),
            jax.ShapeDtypeStruct((PEER_MAX, devices), jnp.int32),
            jax.ShapeDtypeStruct((users + 8, SAMPLES), F32),
        ],
        scratch_shapes=[
            pltpu.VMEM((aps * antennas, 2, users, tones), BF16),
            pltpu.VMEM((2 * tones, 2 * TAPS), BF16),
            pltpu.SemaphoreType.DMA((aps * antennas,)),
            pltpu.SemaphoreType.DMA((3,)),
        ],
        compiler_params=pltpu.CompilerParams(vmem_limit_bytes=LARGE_BYTES),
        cost_estimate=pl.CostEstimate(
            flops=4 * guesses.size * TAPS, bytes_accessed=2 * guesses.size, transcendentals=0
        ),
        name="delay_coefficients",
    )(guesses, table, packed)


def payload_kernel(shape, *refs):
    aps, antennas, users, devices, shards = shape
    per = devices // shards
    parts = refs[:shards]
    table, pick, weights, extras = refs[shards : shards + 4]
    outs = refs[shards + 4 : shards + 4 + per]
    coef, smooth, cov = refs[shards + 4 + per :]

    total = parts[0][...].astype(F32)
    for part in parts[1:]:
        total = total + part[...].astype(F32)
    coef_b = total.astype(BF16)
    coef[:, : 2 * TAPS] = coef_b
    coef[:, 2 * TAPS :] = coef_b

    smooth[...] = jnp.dot(coef[...], table[...], preferred_element_type=F32)
    for a in range(aps):
        base = a * antennas * users
        sums = {}
        for start in range(0, users, 8):
            re, im = [], []
            for i in range(antennas):
                rows = smooth[pl.ds(base + i * users + start, 8), :]
                re.append(rows[:, :SAMPLES])
                im.append(rows[:, SAMPLES:])
            weight = extras[pl.ds(start, 8), :]
            for i in range(antennas):
                sre, sim = re[i] * weight, im[i] * weight
                for j in range(i + 1):
                    value = sre * re[j] + sim * im[j]
                    sums[i, j, 0] = sums[i, j, 0] + value if start else value
                    if j < i:
                        value = sim * re[j] - sre * im[j]
                        sums[i, j, 1] = sums[i, j, 1] + value if start else value
        field = 0
        for i in range(antennas):
            for j in range(i + 1):
                for c in range(2 if j < i else 1):
                    row = jnp.sum(sums[i, j, c], axis=0, keepdims=True)
                    if i == j:
                        row = row + extras[pl.ds(users + a, 1), :]
                    cov[pl.ds(a * antennas * antennas + field, 1), :] = row
                    field += 1

    cov_parts = three_parts(cov[...])
    cov_rows = cov.shape[0]
    first = aps * antennas * ROWS
    for ai in range(aps * antennas):
        chosen = jnp.dot(
            pick[...], coef[pl.ds(ai * users, users), : 2 * TAPS], preferred_element_type=F32
        ).astype(BF16)
        for j in range(per):
            outs[j][pl.ds(ai * ROWS, ROWS), :] = chosen[j * ROWS : (j + 1) * ROWS]
    for j in range(per):
        for k in range(3):
            outs[j][pl.ds(first + k * cov_rows, cov_rows), :] = cov_parts[k]
        outs[j][pl.ds(first + 3 * cov_rows, ROWS), :] = weights[pl.ds(j * ROWS, ROWS), :]


def payload_rows(aps, antennas):
    return aps * antennas * ROWS + 3 * aps * antennas * antennas + ROWS


def owner_payloads(parts, table, pick, weights, extras, shape):
    aps, antennas, users, devices, shards = shape
    per = devices // shards
    rows = payload_rows(aps, antennas)
    operands = list(parts) + [table, pick, weights, extras]
    vmem = pl.BlockSpec(memory_space=pltpu.VMEM)
    return pl.pallas_call(
        functools.partial(payload_kernel, shape),
        in_specs=[vmem] * len(operands),
        out_specs=[vmem] * per,
        out_shape=[jax.ShapeDtypeStruct((rows, 2 * TAPS), BF16)] * per,
        scratch_shapes=[
            pltpu.VMEM((aps * antennas * users, 4 * TAPS), BF16),
            pltpu.VMEM((aps * antennas * users, 2 * SAMPLES), F32),
            pltpu.VMEM((aps * antennas * antennas, SAMPLES), F32),
        ],
        compiler_params=pltpu.CompilerParams(vmem_limit_bytes=SMALL_BYTES),
        cost_estimate=pl.CostEstimate(
            flops=4 * aps * antennas * users * 4 * TAPS * SAMPLES,
            bytes_accessed=2 * 1024 * 1024,
            transcendentals=0,
        ),
        name="owner_payloads",
    )(*operands)


def complex_times(left, right):
    return (left[0] * right[0] - left[1] * right[1], left[0] * right[1] + left[1] * right[0])


def times_conj(left, right):
    return (left[0] * right[0] + left[1] * right[1], left[1] * right[0] - left[0] * right[1])


def minus(left, right):
    return (left[0] - right[0], left[1] - right[1])


def factorize(cov, antennas):
    factor, inverse = {}, []
    for j in range(antennas):
        pivot = cov[j, j][0]
        for k in range(j):
            pivot = pivot - (factor[j, k][0] * factor[j, k][0] + factor[j, k][1] * factor[j, k][1])
        root = lax.rsqrt(pivot)
        inverse.append(root)
        for i in range(j + 1, antennas):
            running = cov[i, j]
            for k in range(j):
                running = minus(running, times_conj(factor[i, k], factor[j, k]))
            factor[i, j] = (running[0] * root, running[1] * root)
    return factor, inverse


def substitute(factor, inverse, right):
    antennas = len(inverse)
    forward = []
    for i in range(antennas):
        running = right[i]
        for k in range(i):
            running = minus(running, complex_times(factor[i, k], forward[k]))
        forward.append((running[0] * inverse[i], running[1] * inverse[i]))
    result = [None] * antennas
    for i in range(antennas - 1, -1, -1):
        running = forward[i]
        for k in range(i + 1, antennas):
            running = minus(running, times_conj(result[k], factor[k, i]))
        result[i] = (running[0] * inverse[i], running[1] * inverse[i])
    return result


def estimate_kernel(shape, chunk, group, slots, *refs):
    aps, antennas, symbols, tones, devices, shards = shape
    count = devices // shards
    first_call, last_call = group == 0, group == shards - 1
    pays, signals = refs[:devices], refs[devices : devices + count]
    refs = refs[devices + count :]
    kernel_table, rebuild_table = refs[:2]
    refs = refs[2:]
    if first_call:
        out, denominator_out = refs[:2]
        refs = refs[2:]
    else:
        acc_in, denominator_in, out = refs[:3]
        refs = refs[3:]
    (
        left, cov_full, cov_tiles, sig_tiles, solved, smooth, weight,
        acc, denominator, turned, staged, out_sem,
    ) = refs
    if first_call:
        acc, denominator = out, denominator_out
    device, core = lax.axis_index("ap"), lax.axis_index("sc")
    cov_rows = aps * antennas * antennas
    coef_rows = aps * antennas * ROWS
    blocks = tones // 128

    dirichlet, rebuild = kernel_table.at[core], rebuild_table.at[core]

    def payload(n, start, size):
        value = pays[n][pl.ds(start, size), :]
        for h in range(1, shards):
            value = jnp.where(
                (core ^ h) == group, pays[h * count + n][pl.ds(start, size), :], value
            )
        return value

    def cov_part(k):
        return jnp.concatenate(
            [payload(n, coef_rows + k * cov_rows, cov_rows) for n in range(count)], axis=0
        )

    high, middle, low = cov_part(0), cov_part(1), cov_part(2)
    n = SAMPLES
    cov_full[...] = (
        jnp.dot(low, dirichlet[:n], preferred_element_type=F32)
        + jnp.dot(
            jnp.concatenate([middle, middle], axis=1), dirichlet[: 2 * n], preferred_element_type=F32
        )
        + jnp.dot(
            jnp.concatenate([high, high, high], axis=1), dirichlet[...], preferred_element_type=F32
        )
    )

    for n in range(count):
        rows = payload(n, 0, coef_rows)
        left[pl.ds(n * coef_rows, coef_rows), : 2 * TAPS] = rows
        left[pl.ds(n * coef_rows, coef_rows), 2 * TAPS :] = rows
        packed = payload(n, coef_rows + 3 * cov_rows, ROWS).astype(F32)
        for a in range(aps):
            value = packed[:, a : a + 1] + packed[:, 8 + a : 9 + a] + packed[:, 16 + a : 17 + a]
            weight[n, a] = jnp.broadcast_to(value, (ROWS, 128))

    if first_call:
        acc[...] = jnp.zeros_like(acc)
        denominator[...] = jnp.ones_like(denominator)
    else:
        acc[...] = acc_in[...]
        denominator[...] = denominator_in[...]

    for n in range(count):
        for a in range(aps):
            for i in range(antennas):
                for c in range(2):
                    rows = signals[n][a, i, c].astype(F32)
                    first = ((a * antennas + i) * 2 + c) * symbols * blocks
                    for b in range(blocks):
                        sig_tiles[n, pl.ds(first + b, symbols, stride=blocks), :] = rows[
                            :, b * 128 : (b + 1) * 128
                        ]

    def solve(l, carry):
        for r in range(0, cov_rows, 8):
            rows = cov_full[pl.ds(pl.multiple_of(l * cov_rows + r, 8), 8), :]
            for b in range(blocks):
                cov_tiles[pl.ds(r * blocks + b, 8, stride=blocks), :] = rows[:, b * 128 : (b + 1) * 128]
        for a in range(aps):
            cov = {}
            field = a * antennas * antennas
            for i in range(antennas):
                for j in range(i + 1):
                    parts = []
                    for c in range(2 if j < i else 1):
                        parts.append(cov_tiles[pl.ds(field * blocks, blocks), :])
                        field += 1
                    cov[i, j] = parts
            factor, inverse = factorize(cov, antennas)
            for s in range(symbols):
                right = []
                for i in range(antennas):
                    tiles = [
                        (((a * antennas + i) * 2 + c) * symbols + s) * blocks for c in range(2)
                    ]
                    right.append([sig_tiles[l, pl.ds(t, blocks), :] for t in tiles])
                result = substitute(factor, inverse, right)
                for i in range(antennas):
                    re, im = result[i]
                    at = ((a * antennas + i) * symbols + s) * 3
                    for c, tile in enumerate((re, im - re, re + im)):
                        solved[l, pl.ds((at + c) * blocks, blocks), :] = tile
        source = (group * count + l) ^ device
        for p in range(PEER_MAX):
            k = slots[p, source]
            for a in range(aps):
                denominator[k] = denominator[k] + weight[l, a, pl.ds(p * CU, CU), :]
        return carry

    lax.fori_loop(0, count, solve, 0)

    def combine(l, q):
        source = (group * count + l) ^ device
        for h in range(chunk // 128):
            b = q * (chunk // 128) + h
            lanes = pl.ds(pl.multiple_of(b * 128, 128), 128)
            totals = [[None] * (3 * symbols) for p in range(PEER_MAX)]
            for a in range(aps):
                for i in range(antennas):
                    base = pl.multiple_of(l * coef_rows + (a * antennas + i) * ROWS, 8)
                    link = []
                    for p in range(PEER_MAX):
                        scale = weight[l, a, pl.ds(p * CU, CU), :]
                        rows = pl.ds(base + p * CU, CU)
                        re = smooth[rows, h * 128 : (h + 1) * 128] * scale
                        im = smooth[rows, chunk + h * 128 : chunk + (h + 1) * 128] * scale
                        link.append((re - im, re, im))
                    for s in range(symbols):
                        at = ((a * antennas + i) * symbols + s) * 3
                        for c in range(3):
                            x = solved[l, pl.ds((at + c) * blocks + b, 1), :]
                            x = jnp.broadcast_to(x, (CU, 128))
                            for p in range(PEER_MAX):
                                value = link[p][c] * x
                                old = totals[p][3 * s + c]
                                totals[p][3 * s + c] = value if old is None else old + value
            for p in range(PEER_MAX):
                k = slots[p, source]
                for s in range(symbols):
                    both, upper, lower = totals[p][3 * s : 3 * s + 3]
                    acc[k, 2 * s, :, lanes] = acc[k, 2 * s, :, lanes] + (both + lower)
                    acc[k, 2 * s + 1, :, lanes] = acc[k, 2 * s + 1, :, lanes] + (both + upper)

    chunks = tones // chunk

    def output_copy(q):
        lanes = pl.ds(pl.multiple_of(q * chunk, 128), chunk)
        return pltpu.make_async_copy(staged.at[q], out.at[:, :, :, :, lanes], out_sem.at[q])

    def finish(q):
        for k in range(OWN_MAX):
            inverse = 1.0 / denominator[k]
            first = k * CU * 2 * symbols
            for h in range(chunk // 128):
                lanes = pl.ds(pl.multiple_of(q * chunk + h * 128, 128), 128)
                for e in range(2 * symbols):
                    value = acc[k, e, :, lanes] * inverse
                    turned[pl.ds(first + e, CU, stride=2 * symbols), :] = value
                for m in range(CU):
                    for s in range(symbols):
                        at = first + (m * symbols + s) * 2
                        staged[q, k, m, s, :, h * 128 : (h + 1) * 128] = turned[pl.ds(at, 2), :]
        output_copy(q).start()

    def one_chunk(q, carry):
        columns = pl.ds(pl.multiple_of(q * 2 * chunk, 128), 2 * chunk)
        smooth[...] = jnp.dot(left[...], rebuild[:, columns], preferred_element_type=F32)

        def step(l, inner):
            combine(l, q)
            return inner

        lax.fori_loop(0, count, step, 0)
        if last_call:
            finish(q)
        return carry

    lax.fori_loop(0, chunks, one_chunk, 0)
    if last_call:
        for q in range(chunks):
            output_copy(q).wait()


def owner_estimates(slots, pays, signals, group, before, shape):
    aps, antennas, symbols, tones, devices, shards = shape
    chunk = min(512, tones // 2)
    count = devices // shards
    last_call = group == shards - 1
    cov_rows = aps * antennas * antennas
    coef_rows = aps * antennas * ROWS
    blocks = tones // 128
    hbm = pl.BlockSpec(memory_space=pltpu.HBM)
    vmem = pl.BlockSpec(memory_space=pltpu.VMEM)
    smem = pl.BlockSpec(memory_space=pltpu.SMEM)
    sums = (OWN_MAX, 2 * symbols, CU, tones)
    bottom = (OWN_MAX, CU, 128)
    if last_call:
        outs = [jax.ShapeDtypeStruct((OWN_MAX, CU, symbols, 2, tones), F32)]
    else:
        outs = [jax.ShapeDtypeStruct(sums, F32), jax.ShapeDtypeStruct(bottom, F32)]
    return pl.pallas_call(
        functools.partial(estimate_kernel, shape, chunk, group),
        in_specs=[smem] + [vmem] * (len(pays) + len(signals) + 2 + len(before)),
        out_specs=[hbm] if last_call else [vmem] * len(outs),
        out_shape=outs,
        scratch_shapes=[
            pltpu.VMEM((count * coef_rows, 4 * TAPS), BF16),
            pltpu.VMEM((count * cov_rows, tones), F32),
            pltpu.VMEM((cov_rows * blocks, 128), F32),
            pltpu.VMEM((count, aps * antennas * 2 * symbols * blocks, 128), F32),
            pltpu.VMEM((count, aps * antennas * 3 * symbols * blocks, 128), F32),
            pltpu.VMEM((count * coef_rows, 2 * chunk), F32),
            pltpu.VMEM((count, aps, ROWS, 128), F32),
            pltpu.VMEM(sums, F32),
            pltpu.VMEM(bottom, F32),
            pltpu.VMEM((CU * 2 * symbols * OWN_MAX, 128), F32),
            pltpu.VMEM((tones // chunk, OWN_MAX, CU, symbols, 2, chunk), F32),
            pltpu.SemaphoreType.DMA((tones // chunk,)),
        ],
        compiler_params=pltpu.CompilerParams(vmem_limit_bytes=VMEM_BYTES),
        cost_estimate=pl.CostEstimate(
            flops=4 * count * coef_rows * 4 * TAPS * tones,
            bytes_accessed=8 * 1024 * 1024,
            transcendentals=0,
        ),
        name="owner_estimates",
    )(
        slots,
        *pays,
        *signals,
        jnp.asarray(dirichlet_tables(shards, tones)),
        jnp.asarray(rebuild_tables(shards, tones, chunk)),
        *before,
    )


def local(
    unsmoothed_link_guesses,
    received,
    user_power,
    noise_power,
    ap_gain,
    user_cluster,
    serving,
    cluster_owner,
):
    aps, antennas, _, users, tones = unsmoothed_link_guesses.shape
    symbols = received.shape[3]
    devices, shards = lax.axis_size("ap"), lax.axis_size("sc")
    per = devices // shards
    def swap_ap(value, v):
        return lax.ppermute(value, "ap", [(i, i ^ v) for i in range(devices)])

    def swap_sc(value, h):
        return lax.ppermute(value, "sc", [(c, c ^ h) for c in range(shards)])

    signals = [None] * devices
    for v in range(0, devices, 2):
        signals[v] = swap_ap(received, v) if v else received
    signals[1] = swap_ap(received, 1)

    combined, samples, pick, weights, slots, extras = delay_coefficients(
        unsmoothed_link_guesses, user_power, noise_power, ap_gain, user_cluster, serving,
        cluster_owner, (aps, antennas, users, devices, shards),
    )
    combined, early = lax.optimization_barrier((combined, [signals[v] for v in EARLY]))
    for v, value in zip(EARLY, early):
        signals[v] = value
    parts = [combined] + [swap_sc(combined, h) for h in range(1, shards)]
    blocks = owner_payloads(
        parts, samples, pick, weights, extras, (aps, antennas, users, devices, shards)
    )

    pairs = lambda j: [
        (i * shards + c, (i ^ (c * per + j)) * shards + c)
        for i in range(devices)
        for c in range(shards)
    ]
    own = [lax.ppermute(blocks[j], ("ap", "sc"), pairs(j)) for j in range(per)]
    pays = own + [swap_sc(own[j], h) for h in range(1, shards) for j in range(per)]
    for v in range(2, devices, 2):
        value = signals[v] if v in EARLY else lax.optimization_barrier((signals[v], own[0]))[0]
        signals[v + 1] = swap_ap(value, 1)
    shape = (aps, antennas, symbols, tones, devices, shards)
    result = []
    for group in range(shards):
        result = owner_estimates(
            slots, pays, signals[group * per : (group + 1) * per], group, result, shape
        )
    return result[0]


def solution(mesh):
    placed = (
        P(("cell", "ap"), None, None, None, "sc"),
        P(("cell", "ap"), None, None, None, "sc"),
        P("cell"),
        P(("cell", "ap")),
        P(("cell", "ap"), None),
        P("cell"),
        P("cell", None),
        P("cell", None),
    )
    return jax.shard_map(
        local,
        mesh=mesh,
        in_specs=placed,
        out_specs=P(("cell", "ap"), None, None, None, "sc"),
        check_vma=False,
    )
```

```python
import functools
import math

import jax
import jax.numpy as jnp
import ml_dtypes
import numpy as np
from jax import lax
from jax.experimental import pallas as pl
from jax.experimental.pallas import tpu as pltpu
from jax.sharding import PartitionSpec as P

TONE_NUMBER = 2048
TAPS = 64
CU = 8
OWN_MAX = 4
PEER_MAX = 2
EARLY = (1, 4)
SAMPLES = 2 * TAPS
ROWS = PEER_MAX * CU
LARGE_BYTES = 52 * 1024 * 1024
SMALL_BYTES = 24 * 1024 * 1024
TABLE_ROWS = 32 * 1024
VMEM_BYTES = 36 * 1024 * 1024
F32 = jnp.float32
BF16 = jnp.bfloat16


def np_parts(values, count):
    parts = []
    rest = values.astype(np.float64)
    for _ in range(count):
        part = rest.astype(np.float32).astype(ml_dtypes.bfloat16)
        parts.append(part)
        rest = rest - part.astype(np.float64)
    return parts


def np_angles(tones):
    turns = (tones[:, None] * np.arange(TAPS)[None, :]) % TONE_NUMBER
    return turns.astype(np.float64) * (2.0 * math.pi / TONE_NUMBER)


def forward_tables(shards, width):
    angles = np_angles(np.arange(shards * width))
    cosine = np.cos(angles).astype(np.float32).astype(ml_dtypes.bfloat16)
    sine = np.sin(angles).astype(np.float32).astype(ml_dtypes.bfloat16)
    real = np.concatenate([cosine, sine], axis=1).reshape(shards, width, 2 * TAPS)
    imag = np.concatenate([-sine, cosine], axis=1).reshape(shards, width, 2 * TAPS)
    return np.stack([real, imag], axis=1)


def rebuild_columns(tones):
    angles = np_angles(tones).T
    real = np.concatenate([np.cos(angles), np.sin(angles)], axis=0)
    imag = np.concatenate([-np.sin(angles), np.cos(angles)], axis=0)
    return (
        np.concatenate(np_parts(real, 2), axis=0),
        np.concatenate(np_parts(imag, 2), axis=0),
    )


def rebuild_tables(shards, width, chunk):
    real, imag = rebuild_columns(np.arange(shards * width))
    real = real.reshape(4 * TAPS, shards, width // chunk, 1, chunk)
    imag = imag.reshape(4 * TAPS, shards, width // chunk, 1, chunk)
    both = np.concatenate([real, imag], axis=3).reshape(4 * TAPS, shards, 2 * width)
    return np.ascontiguousarray(both.transpose(1, 0, 2))


def sample_table():
    real, imag = rebuild_columns(np.arange(SAMPLES) * (TONE_NUMBER // SAMPLES))
    return np.concatenate([real, imag], axis=1)


def first_tables(shards, width):
    forward = forward_tables(shards, width).reshape(shards * 2 * width, 2 * TAPS)
    samples = sample_table()
    rows = np.concatenate([forward, samples[:, :SAMPLES], samples[:, SAMPLES:]], axis=0)
    filling = max(0, TABLE_ROWS - rows.shape[0])
    return np.concatenate([rows, np.zeros((filling, 2 * TAPS), ml_dtypes.bfloat16)], axis=0)


def dirichlet_tables(shards, width):
    step = TONE_NUMBER // SAMPLES
    wave = np.ones((TONE_NUMBER,), np.float64)
    tones = np.arange(TONE_NUMBER)
    for lag in range(1, TAPS):
        wave += 2.0 * np.cos(2.0 * math.pi * ((lag * tones) % TONE_NUMBER) / TONE_NUMBER)
    wave /= SAMPLES
    gap = (np.arange(shards * width)[None, :] - step * np.arange(SAMPLES)[:, None]) % TONE_NUMBER
    kernel = wave[gap]
    parts = np.concatenate(np_parts(kernel, 3), axis=0)
    parts = parts.reshape(3 * SAMPLES, shards, width)
    return np.ascontiguousarray(parts.transpose(1, 0, 2))


def three_parts(values):
    high = values.astype(BF16)
    rest = values - high.astype(F32)
    middle = rest.astype(BF16)
    low = (rest - middle.astype(F32)).astype(BF16)
    return high, middle, low


def iota(shape, axis):
    return lax.broadcasted_iota(jnp.int32, shape, axis)


def column_of(row):
    n = row.shape[1]
    return jnp.sum(jnp.where(iota((n, n), 0) == iota((n, n), 1), row, 0.0), axis=1, keepdims=True)


def row_of(column):
    n = column.shape[0]
    return jnp.sum(
        jnp.where(iota((n, n), 0) == iota((n, n), 1), column, 0.0), axis=0, keepdims=True
    )


def pack_rows(power, noise, gain, cluster, serving, owner):
    width = max(power.shape[0], serving.shape[1], serving.shape[0])
    rows = [
        power[None, :], gain, cluster.astype(F32)[None, :], serving.astype(F32),
        owner.astype(F32).reshape(1, -1), noise[None, :],
    ]
    return jnp.concatenate([jnp.pad(x, ((0, 0), (0, width - x.shape[1]))) for x in rows], axis=0)


def find_routes(shape, clusters, packed, pick_out, weight_out, slots, extras):
    aps, antennas, users, devices, shards = shape
    per = devices // shards
    device, core = lax.axis_index("ap"), lax.axis_index("sc")
    power = packed[pl.ds(0, 1), :][:, :users]
    gain = [packed[pl.ds(1 + a, 1), :][:, :users] for a in range(aps)]
    cluster_row = packed[pl.ds(1 + aps, 1), :][:, :users]
    serving_f = packed[pl.ds(2 + aps, clusters), :][:, : aps * devices]
    owner_row = packed[pl.ds(2 + aps + clusters, 1), :][:, :clusters]
    noise = packed[pl.ds(3 + aps + clusters, 1), :]
    extras[pl.ds(0, users), :] = jnp.broadcast_to(
        column_of(power) * (1.0 / users), (users, SAMPLES)
    )
    for a in range(aps):
        extras[pl.ds(users + a, 1), :] = jnp.broadcast_to(noise[:, a : a + 1], (1, SAMPLES))

    columns = aps * devices
    pairs = (iota((columns, devices), 0) // aps == iota((columns, devices), 1)).astype(F32)
    served = (jnp.dot(serving_f, pairs, preferred_element_type=F32) > 0.5).astype(F32)
    served_here = jnp.sum(
        jnp.where(iota((clusters, devices), 1) == device, served, 0.0), axis=1, keepdims=True
    )
    owner_f = column_of(owner_row)
    owner_col = owner_f.astype(jnp.int32)
    square = (clusters, clusters)
    before = iota(square, 1) < iota(square, 0)
    earlier = before & (owner_f == owner_row)
    turn = jnp.sum(jnp.where(earlier, row_of(served_here), 0.0), axis=1, keepdims=True)
    label = (owner_col ^ device) ^ (core * per)
    valid = (served_here > 0.5) & (label < per)
    base = jnp.where(valid, label.astype(F32) * ROWS + turn * CU, -4.0 * ROWS * devices)
    members = (iota((clusters, users), 0).astype(F32) == cluster_row).astype(F32)
    prefix = (iota((users, users), 0) < iota((users, users), 1)).astype(F32)
    order = jnp.dot(members, prefix, preferred_element_type=F32)
    target = jnp.sum(members * (order + base), axis=0, keepdims=True).astype(jnp.int32)
    pick = (iota((per * ROWS, users), 0) == target).astype(F32).astype(BF16)
    pick_out[...] = pick

    weight_rows = []
    for a in range(aps):
        column = iota((clusters, columns), 1) == device * aps + a
        mine = jnp.sum(jnp.where(column, serving_f, 0.0), axis=1, keepdims=True)
        weight_rows.append(
            jnp.sum(members * mine, axis=0, keepdims=True) * gain[a]
        )
    stacked = jnp.concatenate(weight_rows + [jnp.zeros((8 - aps, users), F32)], axis=0)
    weight_parts = jnp.concatenate(
        [part.astype(F32) for part in three_parts(stacked)]
        + [jnp.zeros((2 * TAPS - 24, users), F32)],
        axis=0,
    ).astype(BF16)
    weight_out[...] = lax.dot_general(
        pick, weight_parts, (((1,), (1,)), ((), ())), preferred_element_type=F32
    ).astype(BF16)

    mine = (owner_col == device).astype(F32)
    rank = jnp.sum(jnp.where(before, row_of(mine), 0.0), axis=1, keepdims=True)
    here = mine * served
    turns = jnp.dot(before.astype(F32), here, preferred_element_type=F32)
    for p in range(PEER_MAX):
        hit = jnp.where(turns == float(p), here, 0.0)
        slots[pl.ds(p, 1), :] = jnp.sum(hit * rank, axis=0, keepdims=True).astype(jnp.int32)


def coefficient_kernel(shape, clusters, *refs):
    aps, antennas, users, devices, shards = shape
    guesses, table, packed = refs[:3]
    out, samples, pick, weights, slots, extras = refs[3:9]
    held, tables, held_sem, table_sem = refs[9:]
    tones = held.shape[-1]
    first = pl.multiple_of(lax.axis_index("sc") * 2 * tones, 16)
    table_copy = pltpu.make_async_copy(table.at[pl.ds(first, 2 * tones)], tables, table_sem.at[0])
    sample_copies = [
        pltpu.make_async_copy(
            table.at[pl.ds(shards * 2 * tones + c * 4 * TAPS, 4 * TAPS)],
            samples.at[:, pl.ds(c * SAMPLES, SAMPLES)],
            table_sem.at[1 + c],
        )
        for c in range(2)
    ]
    big = [
        pltpu.make_async_copy(guesses.at[a, i], held.at[a * antennas + i], held_sem.at[a * antennas + i])
        for a in range(aps)
        for i in range(antennas)
    ]
    for copy in [table_copy] + big + sample_copies:
        copy.start()
    find_routes(shape, clusters, packed, pick, weights, slots, extras)
    table_copy.wait()
    group = math.gcd(2, antennas)
    for first in range(0, aps * antennas, group):
        for k in range(group):
            big[first + k].wait()
        real = held[pl.ds(first, group), 0].reshape(group * users, tones)
        imag = held[pl.ds(first, group), 1].reshape(group * users, tones)
        total = jnp.dot(real, tables[pl.ds(0, tones), :], preferred_element_type=F32)
        total = total + jnp.dot(imag, tables[pl.ds(tones, tones), :], preferred_element_type=F32)
        out[pl.ds(first * users, group * users), :] = (total * (1.0 / TONE_NUMBER)).astype(BF16)
    for copy in sample_copies:
        copy.wait()


def delay_coefficients(guesses, power, noise, gain, cluster, serving, owner, shape):
    aps, antennas, users, devices, shards = shape
    per = devices // shards
    tones = guesses.shape[-1]
    clusters = serving.shape[0]
    table = jnp.asarray(first_tables(shards, tones))
    packed = pack_rows(power, noise, gain, cluster, serving, owner)
    hbm = pl.BlockSpec(memory_space=pltpu.HBM)
    vmem = pl.BlockSpec(memory_space=pltpu.VMEM)
    return pl.pallas_call(
        functools.partial(coefficient_kernel, shape, clusters),
        in_specs=[hbm, hbm, vmem],
        out_specs=[vmem] * 6,
        out_shape=[
            jax.ShapeDtypeStruct((aps * antennas * users, 2 * TAPS), BF16),
            jax.ShapeDtypeStruct((4 * TAPS, 2 * SAMPLES), BF16),
            jax.ShapeDtypeStruct((per * ROWS, users), BF16),
            jax.ShapeDtypeStruct((per * ROWS, 2 * TAPS), BF16),
            jax.ShapeDtypeStruct((PEER_MAX, devices), jnp.int32),
            jax.ShapeDtypeStruct((users + 8, SAMPLES), F32),
        ],
        scratch_shapes=[
            pltpu.VMEM((aps * antennas, 2, users, tones), BF16),
            pltpu.VMEM((2 * tones, 2 * TAPS), BF16),
            pltpu.SemaphoreType.DMA((aps * antennas,)),
            pltpu.SemaphoreType.DMA((3,)),
        ],
        compiler_params=pltpu.CompilerParams(vmem_limit_bytes=LARGE_BYTES),
        cost_estimate=pl.CostEstimate(
            flops=4 * guesses.size * TAPS, bytes_accessed=2 * guesses.size, transcendentals=0
        ),
        name="delay_coefficients",
    )(guesses, table, packed)


def payload_kernel(shape, *refs):
    aps, antennas, users, devices, shards = shape
    per = devices // shards
    parts = refs[:shards]
    table, pick, weights, extras = refs[shards : shards + 4]
    outs = refs[shards + 4 : shards + 4 + per]
    coef, smooth, cov = refs[shards + 4 + per :]

    total = parts[0][...].astype(F32)
    for part in parts[1:]:
        total = total + part[...].astype(F32)
    coef_b = total.astype(BF16)
    coef[:, : 2 * TAPS] = coef_b
    coef[:, 2 * TAPS :] = coef_b

    smooth[...] = jnp.dot(coef[...], table[...], preferred_element_type=F32)
    for a in range(aps):
        base = a * antennas * users
        sums = {}
        for start in range(0, users, 8):
            re, im = [], []
            for i in range(antennas):
                rows = smooth[pl.ds(base + i * users + start, 8), :]
                re.append(rows[:, :SAMPLES])
                im.append(rows[:, SAMPLES:])
            weight = extras[pl.ds(start, 8), :]
            for i in range(antennas):
                sre, sim = re[i] * weight, im[i] * weight
                for j in range(i + 1):
                    value = sre * re[j] + sim * im[j]
                    sums[i, j, 0] = sums[i, j, 0] + value if start else value
                    if j < i:
                        value = sim * re[j] - sre * im[j]
                        sums[i, j, 1] = sums[i, j, 1] + value if start else value
        field = 0
        for i in range(antennas):
            for j in range(i + 1):
                for c in range(2 if j < i else 1):
                    row = jnp.sum(sums[i, j, c], axis=0, keepdims=True)
                    if i == j:
                        row = row + extras[pl.ds(users + a, 1), :]
                    cov[pl.ds(a * antennas * antennas + field, 1), :] = row
                    field += 1

    cov_parts = three_parts(cov[...])
    cov_rows = cov.shape[0]
    first = aps * antennas * ROWS
    for ai in range(aps * antennas):
        chosen = jnp.dot(
            pick[...], coef[pl.ds(ai * users, users), : 2 * TAPS], preferred_element_type=F32
        ).astype(BF16)
        for j in range(per):
            outs[j][pl.ds(ai * ROWS, ROWS), :] = chosen[j * ROWS : (j + 1) * ROWS]
    for j in range(per):
        for k in range(3):
            outs[j][pl.ds(first + k * cov_rows, cov_rows), :] = cov_parts[k]
        outs[j][pl.ds(first + 3 * cov_rows, ROWS), :] = weights[pl.ds(j * ROWS, ROWS), :]


def payload_rows(aps, antennas):
    return aps * antennas * ROWS + 3 * aps * antennas * antennas + ROWS


def owner_payloads(parts, table, pick, weights, extras, shape):
    aps, antennas, users, devices, shards = shape
    per = devices // shards
    rows = payload_rows(aps, antennas)
    operands = list(parts) + [table, pick, weights, extras]
    vmem = pl.BlockSpec(memory_space=pltpu.VMEM)
    return pl.pallas_call(
        functools.partial(payload_kernel, shape),
        in_specs=[vmem] * len(operands),
        out_specs=[vmem] * per,
        out_shape=[jax.ShapeDtypeStruct((rows, 2 * TAPS), BF16)] * per,
        scratch_shapes=[
            pltpu.VMEM((aps * antennas * users, 4 * TAPS), BF16),
            pltpu.VMEM((aps * antennas * users, 2 * SAMPLES), F32),
            pltpu.VMEM((aps * antennas * antennas, SAMPLES), F32),
        ],
        compiler_params=pltpu.CompilerParams(vmem_limit_bytes=SMALL_BYTES),
        cost_estimate=pl.CostEstimate(
            flops=4 * aps * antennas * users * 4 * TAPS * SAMPLES,
            bytes_accessed=2 * 1024 * 1024,
            transcendentals=0,
        ),
        name="owner_payloads",
    )(*operands)


def complex_times(left, right):
    return (left[0] * right[0] - left[1] * right[1], left[0] * right[1] + left[1] * right[0])


def times_conj(left, right):
    return (left[0] * right[0] + left[1] * right[1], left[1] * right[0] - left[0] * right[1])


def minus(left, right):
    return (left[0] - right[0], left[1] - right[1])


def factorize(cov, antennas):
    factor, inverse = {}, []
    for j in range(antennas):
        pivot = cov[j, j][0]
        for k in range(j):
            pivot = pivot - (factor[j, k][0] * factor[j, k][0] + factor[j, k][1] * factor[j, k][1])
        root = lax.rsqrt(pivot)
        inverse.append(root)
        for i in range(j + 1, antennas):
            running = cov[i, j]
            for k in range(j):
                running = minus(running, times_conj(factor[i, k], factor[j, k]))
            factor[i, j] = (running[0] * root, running[1] * root)
    return factor, inverse


def substitute(factor, inverse, right):
    antennas = len(inverse)
    forward = []
    for i in range(antennas):
        running = right[i]
        for k in range(i):
            running = minus(running, complex_times(factor[i, k], forward[k]))
        forward.append((running[0] * inverse[i], running[1] * inverse[i]))
    result = [None] * antennas
    for i in range(antennas - 1, -1, -1):
        running = forward[i]
        for k in range(i + 1, antennas):
            running = minus(running, times_conj(result[k], factor[k, i]))
        result[i] = (running[0] * inverse[i], running[1] * inverse[i])
    return result


def estimate_kernel(shape, chunk, group, slots, *refs):
    aps, antennas, symbols, tones, devices, shards = shape
    count = devices // shards
    first_call, last_call = group == 0, group == shards - 1
    pays, signals = refs[:devices], refs[devices : devices + count]
    refs = refs[devices + count :]
    kernel_table, rebuild_table = refs[:2]
    refs = refs[2:]
    if first_call:
        out, denominator_out = refs[:2]
        refs = refs[2:]
    else:
        acc_in, denominator_in, out = refs[:3]
        refs = refs[3:]
    (
        left, cov_full, cov_tiles, sig_tiles, solved, smooth, weight,
        acc, denominator, turned, staged, out_sem,
    ) = refs
    if first_call:
        acc, denominator = out, denominator_out
    device, core = lax.axis_index("ap"), lax.axis_index("sc")
    cov_rows = aps * antennas * antennas
    coef_rows = aps * antennas * ROWS
    blocks = tones // 128

    dirichlet, rebuild = kernel_table.at[core], rebuild_table.at[core]

    def payload(n, start, size):
        value = pays[n][pl.ds(start, size), :]
        for h in range(1, shards):
            value = jnp.where(
                (core ^ h) == group, pays[h * count + n][pl.ds(start, size), :], value
            )
        return value

    def cov_part(k):
        return jnp.concatenate(
            [payload(n, coef_rows + k * cov_rows, cov_rows) for n in range(count)], axis=0
        )

    high, middle, low = cov_part(0), cov_part(1), cov_part(2)
    n = SAMPLES
    cov_full[...] = (
        jnp.dot(low, dirichlet[:n], preferred_element_type=F32)
        + jnp.dot(
            jnp.concatenate([middle, middle], axis=1), dirichlet[: 2 * n], preferred_element_type=F32
        )
        + jnp.dot(
            jnp.concatenate([high, high, high], axis=1), dirichlet[...], preferred_element_type=F32
        )
    )

    for n in range(count):
        rows = payload(n, 0, coef_rows)
        left[pl.ds(n * coef_rows, coef_rows), : 2 * TAPS] = rows
        left[pl.ds(n * coef_rows, coef_rows), 2 * TAPS :] = rows
        packed = payload(n, coef_rows + 3 * cov_rows, ROWS).astype(F32)
        for a in range(aps):
            value = packed[:, a : a + 1] + packed[:, 8 + a : 9 + a] + packed[:, 16 + a : 17 + a]
            weight[n, a] = jnp.broadcast_to(value, (ROWS, 128))

    if first_call:
        acc[...] = jnp.zeros_like(acc)
        denominator[...] = jnp.ones_like(denominator)
    else:
        acc[...] = acc_in[...]
        denominator[...] = denominator_in[...]

    for n in range(count):
        for a in range(aps):
            for i in range(antennas):
                for c in range(2):
                    rows = signals[n][a, i, c].astype(F32)
                    first = ((a * antennas + i) * 2 + c) * symbols * blocks
                    for b in range(blocks):
                        sig_tiles[n, pl.ds(first + b, symbols, stride=blocks), :] = rows[
                            :, b * 128 : (b + 1) * 128
                        ]

    def solve(l, carry):
        for r in range(0, cov_rows, 8):
            rows = cov_full[pl.ds(pl.multiple_of(l * cov_rows + r, 8), 8), :]
            for b in range(blocks):
                cov_tiles[pl.ds(r * blocks + b, 8, stride=blocks), :] = rows[:, b * 128 : (b + 1) * 128]
        for a in range(aps):
            cov = {}
            field = a * antennas * antennas
            for i in range(antennas):
                for j in range(i + 1):
                    parts = []
                    for c in range(2 if j < i else 1):
                        parts.append(cov_tiles[pl.ds(field * blocks, blocks), :])
                        field += 1
                    cov[i, j] = parts
            factor, inverse = factorize(cov, antennas)
            for s in range(symbols):
                right = []
                for i in range(antennas):
                    tiles = [
                        (((a * antennas + i) * 2 + c) * symbols + s) * blocks for c in range(2)
                    ]
                    right.append([sig_tiles[l, pl.ds(t, blocks), :] for t in tiles])
                result = substitute(factor, inverse, right)
                for i in range(antennas):
                    re, im = result[i]
                    at = ((a * antennas + i) * symbols + s) * 3
                    for c, tile in enumerate((re, im - re, re + im)):
                        solved[l, pl.ds((at + c) * blocks, blocks), :] = tile
        source = (group * count + l) ^ device
        for p in range(PEER_MAX):
            k = slots[p, source]
            for a in range(aps):
                denominator[k] = denominator[k] + weight[l, a, pl.ds(p * CU, CU), :]
        return carry

    lax.fori_loop(0, count, solve, 0)

    def combine(l, q):
        source = (group * count + l) ^ device
        for h in range(chunk // 128):
            b = q * (chunk // 128) + h
            lanes = pl.ds(pl.multiple_of(b * 128, 128), 128)
            totals = [[None] * (3 * symbols) for p in range(PEER_MAX)]
            for a in range(aps):
                for i in range(antennas):
                    base = pl.multiple_of(l * coef_rows + (a * antennas + i) * ROWS, 8)
                    link = []
                    for p in range(PEER_MAX):
                        scale = weight[l, a, pl.ds(p * CU, CU), :]
                        rows = pl.ds(base + p * CU, CU)
                        re = smooth[rows, h * 128 : (h + 1) * 128] * scale
                        im = smooth[rows, chunk + h * 128 : chunk + (h + 1) * 128] * scale
                        link.append((re - im, re, im))
                    for s in range(symbols):
                        at = ((a * antennas + i) * symbols + s) * 3
                        for c in range(3):
                            x = solved[l, pl.ds((at + c) * blocks + b, 1), :]
                            x = jnp.broadcast_to(x, (CU, 128))
                            for p in range(PEER_MAX):
                                value = link[p][c] * x
                                old = totals[p][3 * s + c]
                                totals[p][3 * s + c] = value if old is None else old + value
            for p in range(PEER_MAX):
                k = slots[p, source]
                for s in range(symbols):
                    both, upper, lower = totals[p][3 * s : 3 * s + 3]
                    acc[k, 2 * s, :, lanes] = acc[k, 2 * s, :, lanes] + (both + lower)
                    acc[k, 2 * s + 1, :, lanes] = acc[k, 2 * s + 1, :, lanes] + (both + upper)

    chunks = tones // chunk

    def output_copy(q):
        lanes = pl.ds(pl.multiple_of(q * chunk, 128), chunk)
        return pltpu.make_async_copy(staged.at[q], out.at[:, :, :, :, lanes], out_sem.at[q])

    def finish(q):
        for k in range(OWN_MAX):
            inverse = 1.0 / denominator[k]
            first = k * CU * 2 * symbols
            for h in range(chunk // 128):
                lanes = pl.ds(pl.multiple_of(q * chunk + h * 128, 128), 128)
                for e in range(2 * symbols):
                    value = acc[k, e, :, lanes] * inverse
                    turned[pl.ds(first + e, CU, stride=2 * symbols), :] = value
                for m in range(CU):
                    for s in range(symbols):
                        at = first + (m * symbols + s) * 2
                        staged[q, k, m, s, :, h * 128 : (h + 1) * 128] = turned[pl.ds(at, 2), :]
        output_copy(q).start()

    def one_chunk(q, carry):
        columns = pl.ds(pl.multiple_of(q * 2 * chunk, 128), 2 * chunk)
        smooth[...] = jnp.dot(left[...], rebuild[:, columns], preferred_element_type=F32)

        def step(l, inner):
            combine(l, q)
            return inner

        lax.fori_loop(0, count, step, 0)
        if last_call:
            finish(q)
        return carry

    lax.fori_loop(0, chunks, one_chunk, 0)
    if last_call:
        for q in range(chunks):
            output_copy(q).wait()


def owner_estimates(slots, pays, signals, group, before, shape):
    aps, antennas, symbols, tones, devices, shards = shape
    chunk = min(512, tones // 2)
    count = devices // shards
    last_call = group == shards - 1
    cov_rows = aps * antennas * antennas
    coef_rows = aps * antennas * ROWS
    blocks = tones // 128
    hbm = pl.BlockSpec(memory_space=pltpu.HBM)
    vmem = pl.BlockSpec(memory_space=pltpu.VMEM)
    smem = pl.BlockSpec(memory_space=pltpu.SMEM)
    sums = (OWN_MAX, 2 * symbols, CU, tones)
    bottom = (OWN_MAX, CU, 128)
    if last_call:
        outs = [jax.ShapeDtypeStruct((OWN_MAX, CU, symbols, 2, tones), F32)]
    else:
        outs = [jax.ShapeDtypeStruct(sums, F32), jax.ShapeDtypeStruct(bottom, F32)]
    return pl.pallas_call(
        functools.partial(estimate_kernel, shape, chunk, group),
        in_specs=[smem] + [vmem] * (len(pays) + len(signals) + 2 + len(before)),
        out_specs=[hbm] if last_call else [vmem] * len(outs),
        out_shape=outs,
        scratch_shapes=[
            pltpu.VMEM((count * coef_rows, 4 * TAPS), BF16),
            pltpu.VMEM((count * cov_rows, tones), F32),
            pltpu.VMEM((cov_rows * blocks, 128), F32),
            pltpu.VMEM((count, (aps * antennas * 2 * symbols + CU) * blocks, 128), F32),
            pltpu.VMEM((count, aps * antennas * 3 * symbols * blocks, 128), F32),
            pltpu.VMEM((count * coef_rows, 2 * chunk), F32),
            pltpu.VMEM((count, aps, ROWS, 128), F32),
            pltpu.VMEM(sums, F32),
            pltpu.VMEM(bottom, F32),
            pltpu.VMEM((CU * 2 * symbols * OWN_MAX, 128), F32),
            pltpu.VMEM((tones // chunk, OWN_MAX, CU, symbols, 2, chunk), F32),
            pltpu.SemaphoreType.DMA((tones // chunk,)),
        ],
        compiler_params=pltpu.CompilerParams(vmem_limit_bytes=VMEM_BYTES),
        cost_estimate=pl.CostEstimate(
            flops=4 * count * coef_rows * 4 * TAPS * tones,
            bytes_accessed=8 * 1024 * 1024,
            transcendentals=0,
        ),
        name="owner_estimates",
    )(
        slots,
        *pays,
        *signals,
        jnp.asarray(dirichlet_tables(shards, tones)),
        jnp.asarray(rebuild_tables(shards, tones, chunk)),
        *before,
    )


def local(
    unsmoothed_link_guesses,
    received,
    user_power,
    noise_power,
    ap_gain,
    user_cluster,
    serving,
    cluster_owner,
):
    aps, antennas, _, users, tones = unsmoothed_link_guesses.shape
    symbols = received.shape[3]
    devices, shards = lax.axis_size("ap"), lax.axis_size("sc")
    per = devices // shards
    def swap_ap(value, v):
        return lax.ppermute(value, "ap", [(i, i ^ v) for i in range(devices)])

    def swap_sc(value, h):
        return lax.ppermute(value, "sc", [(c, c ^ h) for c in range(shards)])

    signals = [None] * devices
    for v in range(0, devices, 2):
        signals[v] = swap_ap(received, v) if v else received
    signals[1] = swap_ap(received, 1)

    combined, samples, pick, weights, slots, extras = delay_coefficients(
        unsmoothed_link_guesses, user_power, noise_power, ap_gain, user_cluster, serving,
        cluster_owner, (aps, antennas, users, devices, shards),
    )
    combined, early = lax.optimization_barrier((combined, [signals[v] for v in EARLY]))
    for v, value in zip(EARLY, early):
        signals[v] = value
    parts = [combined] + [swap_sc(combined, h) for h in range(1, shards)]
    blocks = owner_payloads(
        parts, samples, pick, weights, extras, (aps, antennas, users, devices, shards)
    )

    pairs = lambda j: [
        (i * shards + c, (i ^ (c * per + j)) * shards + c)
        for i in range(devices)
        for c in range(shards)
    ]
    own = [lax.ppermute(blocks[j], ("ap", "sc"), pairs(j)) for j in range(per)]
    pays = own + [swap_sc(own[j], h) for h in range(1, shards) for j in range(per)]
    for v in range(2, devices, 2):
        value = signals[v] if v in EARLY else lax.optimization_barrier((signals[v], own[0]))[0]
        signals[v + 1] = swap_ap(value, 1)
    shape = (aps, antennas, symbols, tones, devices, shards)
    result = []
    for group in range(shards):
        result = owner_estimates(
            slots, pays, signals[group * per : (group + 1) * per], group, result, shape
        )
    return result[0]


def solution(mesh):
    placed = (
        P(("cell", "ap"), None, None, None, "sc"),
        P(("cell", "ap"), None, None, None, "sc"),
        P("cell"),
        P(("cell", "ap")),
        P(("cell", "ap"), None),
        P("cell"),
        P("cell", None),
        P("cell", None),
    )
    return jax.shard_map(
        local,
        mesh=mesh,
        in_specs=placed,
        out_specs=P(("cell", "ap"), None, None, None, "sc"),
        check_vma=False,
    )
```
